32 devices in a mesh: shard: 8 (over z, x), tensor: 4 (over y, core).
Axes of the slice: x: 2, y: 2, z: 4, core: 2. Of those that a mesh axis runs over, the one named last changes fastest.
Arguments:
- gradients: bfloat16 [3, 1152, 6912], P(None, 'shard', 'tensor'), may hold values from -6 to 6
- weights: float32 [3, 1152, 6912], P(None, 'shard', 'tensor'), may hold values from -6 to 6
- projectors: bfloat16 [1152, 3, 256], replicated, may hold values from -0.1875 to 0.1875
- first_moment: float32 [3, 256, 4, 1728], P(None, None, 'tensor', 'shard'), may hold values from -3 to 3
- second_moment: float32 [3, 256, 4, 1728], P(None, None, 'tensor', 'shard'), may hold values from 0.05 to 4
Outputs:
- new_weight: float32 [3, 1152, 6912], P(None, 'shard', 'tensor')
- new_first: float32 [3, 256, 4, 1728], P(None, None, 'tensor', 'shard')
- new_second: float32 [3, 256, 4, 1728], P(None, None, 'tensor', 'shard')
- new_basis: bfloat16 [1152, 3, 256], replicated
The draws below stay inside these ranges and needn't reach their ends.
All inputs are finite; a program needn't handle non-finite values.
Results may differ from the reference program's by a relative error of at most 0.001.
The reference program's roundings to bfloat16 on the way (of `update` and `back`) count: a program that leaves them out, or rounds other values in their place, can miss the bound.
Values may be sent and summed in bfloat16 or wider, within the bound.
No kernel may reach another device: no remote copies, remote signals or barrier semaphores. Data moves between devices by JAX's collectives and lax.ppermute only.
A program may use at most 64 MiB of HBM per device.

```python
import math
import jax
import jax.numpy as jnp
from jax import lax

D = 1152
FF = 6912
R = 256
MATS = 3
NS_STEPS = 5
N_TENSOR = 4


def level_of(own_key, shape, split, smallest, high):
    gain, own = 1.0, jax.random.fold_in(own_key, 6)
    for position, parts in split:
        draws = jnp.exp(jax.random.uniform(jax.random.fold_in(own, position), (parts,), jnp.float32, smallest / len(split), high / len(split)))
        gain = gain * jnp.repeat(draws, shape[position] // parts).reshape([-1 if axis == position else 1 for axis in range(len(shape))])
    return gain


def bell_draw(rng, shape, width, bound, shards=(), kind=jnp.bfloat16):
    gain = level_of(rng, shape, shards, -0.22, 0.18) if shards else 1.0
    drawn = jax.random.normal(rng, shape, jnp.float32) * width * gain
    return jnp.minimum(jnp.maximum(drawn, -bound), bound).astype(kind)


def setup_inputs(seed: int = 0) -> dict:
    splits = jax.random.split(jax.random.key(seed), 6)
    return {
        "gradients": bell_draw(splits[0], (MATS, D, FF), 1.0, 6.0, ((1, 8), (2, 4))),
        "weights": bell_draw(splits[1], (MATS, D, FF), 1.0, 6.0, ((1, 8), (2, 4)), jnp.float32),
        "projectors": bell_draw(splits[2], (D, MATS, R), D ** -0.5, 0.1875),
        "first_moment": bell_draw(splits[3], (MATS, R, N_TENSOR, FF // N_TENSOR), 0.3, 3.0, ((2, 4), (3, 8)), jnp.float32),
        "second_moment": jnp.clip(jnp.exp(math.log(4.0) - 4.3820266 * jax.random.uniform(splits[4], (MATS, R, N_TENSOR, FF // N_TENSOR), jnp.float32) ** level_of(splits[4], (MATS, R, N_TENSOR, FF // N_TENSOR), ((2, 4), (3, 8)), -0.2, 0.2)), 0.05, 4.0),
    }


corr_first = 1.0
corr_second = 0.6323045752

def reference(gradients, weights, projectors, first_moment, second_moment):
    first_whole = first_moment.reshape(MATS, R, FF)
    second_whole = second_moment.reshape(MATS, R, FF)
    weight_list = []
    first_list = []
    second_list = []
    basis_list = []
    for index in range(MATS):
        grad_mat = gradients[index]
        basis_mat = projectors[:, index, :]
        projected = jnp.dot(basis_mat.T, grad_mat, preferred_element_type=jnp.float32)
        first_new = 0.9 * first_whole[index] + 0.1 * projected
        second_new = 0.999 * second_whole[index] + 0.001 * projected * projected
        update = (first_new / corr_first / (jnp.sqrt(second_new / corr_second) + 1e-08)).astype(jnp.bfloat16)
        delta = jnp.dot(basis_mat, update, preferred_element_type=jnp.float32)
        weight_list.append(weights[index] - 0.2 * delta)
        first_list.append(first_new)
        second_list.append(second_new)
        back = jnp.dot(grad_mat.T, basis_mat, preferred_element_type=jnp.float32).astype(jnp.bfloat16)
        refresh = jnp.dot(grad_mat, back, preferred_element_type=jnp.float32)
        iterate = refresh / jnp.sqrt(jnp.sum(refresh * refresh) + 1e-06)
        for sweep in range(NS_STEPS):
            inner = jnp.dot(iterate.T, iterate, precision=lax.Precision.HIGHEST, preferred_element_type=jnp.float32)
            iterate = 1.5 * iterate - 0.5 * jnp.dot(iterate, inner, precision=lax.Precision.HIGHEST, preferred_element_type=jnp.float32)
        basis_list.append((iterate * math.sqrt(D)).astype(jnp.bfloat16))
    shape_four = (MATS, R, N_TENSOR, FF // N_TENSOR)
    return (jnp.stack(weight_list), jnp.stack(first_list).reshape(shape_four), jnp.stack(second_list).reshape(shape_four), jnp.stack(basis_list, axis=1))
```

```python
import functools
import math

import jax
import jax.numpy as jnp
from jax import lax
from jax.experimental import pallas as pl
from jax.experimental.pallas import tpu as pltpu
from jax.sharding import PartitionSpec as P

NS_STEPS = 5
CORR_FIRST = 1.0
CORR_SECOND = 0.6323045752
HIGHEST = lax.Precision.HIGHEST
VMEM = pl.BlockSpec(memory_space=pltpu.VMEM)
PARAMS = pltpu.CompilerParams(vmem_limit_bytes=32 * 1024 * 1024)


def dot(a, b, dims, **kw):
    return lax.dot_general(a, b, (dims, ((), ())), preferred_element_type=jnp.float32, **kw)


def nn(a, b, **kw):
    return dot(a, b, ((1,), (0,)), **kw)


def tn(a, b, **kw):
    return dot(a, b, ((0,), (0,)), **kw)


def nt(a, b, **kw):
    return dot(a, b, ((1,), (1,)), **kw)


def row_owner():
    tensor = lax.axis_index("tensor")
    return (tensor & 1) * 4 + (tensor >> 1) * 2 + (lax.axis_index("shard") & 1)


def pack_kernel(parts, cols, g_ref, *refs):
    outs, held = refs[:parts], refs[parts]
    rows, wide = held.shape[1:]
    for part in range(parts):
        held[part, :, :cols] = g_ref[0, :, part * cols : (part + 1) * cols]
        held[part, :, cols:] = jnp.zeros((rows, wide - cols), held.dtype)
    me = lax.axis_index("shard")
    for k in range(parts):
        outs[k][...] = held[me ^ k]


def pack(gradients, mat, parts, cols, wide):
    _, rows, whole = gradients.shape
    return pl.pallas_call(
        functools.partial(pack_kernel, parts, cols),
        grid=(1,),
        in_specs=[pl.BlockSpec((1, rows, whole), lambda i: (mat, 0, 0))],
        out_specs=[pl.BlockSpec((rows, wide), lambda i: (0, 0))] * parts,
        out_shape=[jax.ShapeDtypeStruct((rows, wide), gradients.dtype)] * parts,
        scratch_shapes=[pltpu.VMEM((parts, rows, wide), gradients.dtype)],
        compiler_params=PARAMS,
        name="cut_columns",
    )(gradients)


def project_kernel(parts, cols, *refs):
    blocks, (p_ref, first_ref, second_ref), refs = refs[:parts], refs[parts : parts + 3], refs[parts + 3 :]
    update_ref, first_out, second_out, send_ref, keep_ref, grad = refs[-6:]
    rows = blocks[0].shape[0]
    me = lax.axis_index("shard")
    for k in range(parts):
        grad[pl.ds(pl.multiple_of((me ^ k) * rows, rows), rows), :] = blocks[k][...]
    projected = tn(grad[...], p_ref[0])
    back = projected.astype(jnp.bfloat16)
    own = row_owner()
    half = parts // 2
    for j in list(range(half, parts)) + list(range(half)):
        at = pl.multiple_of((own ^ j) * rows, rows)
        term = nn(grad[pl.ds(at, rows), :], back)
        out = send_ref if j >= half else keep_ref
        out[(j % half) * rows : (j % half + 1) * rows, :] = term
    projected = projected[:cols]
    first_new = 0.9 * first_ref[0] + 0.1 * projected
    second_new = 0.999 * second_ref[0] + 0.001 * projected * projected
    first_out[0] = first_new
    second_out[0] = second_new
    update_ref[...] = (
        first_new / CORR_FIRST / (jnp.sqrt(second_new / CORR_SECOND) + 1e-08)
    ).astype(jnp.bfloat16)


def project(blocks, projectors, first, second, mat, earlier):
    parts = len(blocks)
    rows, wide = blocks[0].shape
    mats, width, rank = projectors.shape
    cols = first.shape[1]
    moment = pl.BlockSpec((1, cols, rank), lambda i: (mat, 0, 0))
    whole = lambda *shape: pl.BlockSpec(shape, lambda i: (0,) * len(shape))
    in_specs = [whole(rows, wide)] * parts
    in_specs += [pl.BlockSpec((1, width, rank), lambda i: (mat, 0, 0)), moment, moment]
    in_specs += [pl.BlockSpec(memory_space=pl.ANY)] * len(earlier)
    half = width // 2
    return pl.pallas_call(
        functools.partial(project_kernel, parts, cols),
        grid=(1,),
        in_specs=in_specs,
        out_specs=[whole(cols, rank), moment, moment, whole(half, rank), whole(half, rank)],
        out_shape=[
            jax.ShapeDtypeStruct((cols, rank), jnp.bfloat16),
            jax.ShapeDtypeStruct(first.shape, first.dtype),
            jax.ShapeDtypeStruct(second.shape, second.dtype),
            jax.ShapeDtypeStruct((half, rank), jnp.float32),
            jax.ShapeDtypeStruct((half, rank), jnp.float32),
        ],
        scratch_shapes=[pltpu.VMEM((width, wide), jnp.bfloat16)],
        input_output_aliases={parts + 3 + i: 1 + i for i in range(len(earlier))},
        compiler_params=PARAMS,
        name="project",
    )(*blocks, projectors, first, second, *earlier)


def basis_kernel(factor, low_ref, high_ref, *refs):
    out_ref = refs[-1]
    half, rank = low_ref.shape
    rows = half // 4
    low, high = low_ref[...], high_ref[...]
    norm = jnp.sqrt(jnp.sum(low * low) + jnp.sum(high * high) + 1e-06)
    low, high = low / norm, high / norm
    gram = tn(low, low, precision=HIGHEST) + tn(high, high, precision=HIGHEST)
    eye = (
        lax.broadcasted_iota(jnp.int32, (rank, rank), 0)
        == lax.broadcasted_iota(jnp.int32, (rank, rank), 1)
    ).astype(jnp.float32)
    total = None
    for sweep in range(NS_STEPS):
        step = 1.5 * eye - 0.5 * gram
        total = step if total is None else nn(total, step, precision=HIGHEST)
        if sweep < NS_STEPS - 1:
            gram = nn(nn(gram, step, precision=HIGHEST), step, precision=HIGHEST)
    own = row_owner()
    for j in range(8):
        source = low if j < 4 else high
        block = nn(source[(j % 4) * rows : (j % 4 + 1) * rows], total, precision=HIGHEST)
        at = pl.multiple_of((own ^ j) * rows, rows)
        out_ref[0, pl.ds(at, rows), :] = (block * factor).astype(jnp.bfloat16)


def basis(low, high, mat, mats, factor, earlier):
    half, rank = low.shape
    whole = lambda *shape: pl.BlockSpec(shape, lambda i: (0,) * len(shape))
    return pl.pallas_call(
        functools.partial(basis_kernel, factor),
        grid=(1,),
        in_specs=[whole(half, rank)] * 2 + [pl.BlockSpec(memory_space=pl.ANY)] * len(earlier),
        out_specs=pl.BlockSpec((1, 2 * half, rank), lambda i: (mat, 0, 0)),
        out_shape=jax.ShapeDtypeStruct((mats, 2 * half, rank), jnp.bfloat16),
        input_output_aliases={2: 0} if earlier else {},
        compiler_params=PARAMS,
        name="newton_schulz",
    )(low, high, *earlier)


def weight_kernel(cols, w_ref, p_ref, u_ref, out_ref):
    rows = w_ref.shape[1]
    at = pl.multiple_of(lax.axis_index("shard") * rows, rows)
    own = p_ref[0, pl.ds(at, rows), :]
    for part in range(u_ref.shape[0]):
        span = slice(part * cols, (part + 1) * cols)
        out_ref[0, :, span] = w_ref[0, :, span] - 0.2 * nt(own, u_ref[part, 0])


def weight_step(weights, projectors, updates):
    mats, rows, whole = weights.shape
    parts, _, cols, rank = updates.shape
    width = projectors.shape[1]
    big = pl.BlockSpec((1, rows, whole), lambda m: (m, 0, 0))
    return pl.pallas_call(
        functools.partial(weight_kernel, cols),
        grid=(mats,),
        in_specs=[
            big,
            pl.BlockSpec((1, width, rank), lambda m: (m, 0, 0)),
            pl.BlockSpec((parts, 1, cols, rank), lambda m: (0, m, 0, 0)),
        ],
        out_specs=big,
        out_shape=jax.ShapeDtypeStruct(weights.shape, weights.dtype),
        compiler_params=PARAMS,
        name="weight_step",
    )(weights, projectors, updates)


def swap(x, axis, size, bit):
    return lax.ppermute(x, axis, [(i, i ^ bit) for i in range(size)])


def per_device(n_shard, n_tensor, gradients, weights, projectors, first_moment, second_moment):
    factor = math.sqrt(projectors.shape[0])
    mats, rows, whole = gradients.shape
    cols = whole // n_shard
    wide = -(-cols // 128) * 128
    across = jnp.swapaxes(projectors, 0, 1)
    first = jnp.swapaxes(first_moment[:, :, 0, :], 1, 2)
    second = jnp.swapaxes(second_moment[:, :, 0, :], 1, 2)
    core = lambda x: swap(x, "tensor", n_tensor, 1)
    along_y = lambda x: swap(x, "tensor", n_tensor, 2)
    along_x = lambda x: swap(x, "shard", n_shard, 1)
    z_far = lambda x: swap(x, "shard", n_shard, 4)
    z_near = lambda x: swap(x, "shard", n_shard, 2)

    blocks = []
    for mat in range(mats):
        cut = pack(gradients, mat, n_shard, cols, wide)
        blocks.append([cut[0]] + [swap(cut[k], "shard", n_shard, k) for k in range(1, n_shard)])
    moments, bases, updates = (), (), []
    for mat in range(mats):
        update, *moments, send, keep = project(blocks[mat], across, first, second, mat, moments)
        updates.append(update)
        for exchange in (core, along_y, along_x):
            got = exchange(send)
            if keep.shape[0] > rows:
                half = keep.shape[0] // 2
                send, keep = keep[half:] + got[half:], keep[:half] + got[:half]
            else:
                keep = keep + got
        keep = keep + z_far(keep)
        keep = keep + z_near(keep)
        keep = jnp.concatenate([keep, along_x(keep)])
        keep = jnp.concatenate([keep, along_y(keep)])
        bases = (basis(keep, core(keep), mat, mats, factor, bases),)
    gathered = lax.all_gather(jnp.stack(updates), "shard")
    new_weight = weight_step(weights, across, gathered)
    back = lambda x: jnp.swapaxes(x, 1, 2)[:, :, None, :]
    return (new_weight, back(moments[0]), back(moments[1]), jnp.swapaxes(bases[0], 0, 1))


def newton_steps(iterate, inner):
    return 1.5 * iterate - 0.5 * jnp.einsum(
        "dmr,mrs->dms", iterate, inner, precision=HIGHEST, preferred_element_type=jnp.float32
    )


def column_inner(iterate):
    return jnp.einsum(
        "dmr,dms->mrs", iterate, iterate, precision=HIGHEST, preferred_element_type=jnp.float32
    )


def per_device_any(gradients, weights, projectors, first_moment, second_moment):
    factor = math.sqrt(projectors.shape[0])
    regrouped = lax.all_to_all(gradients, "shard", split_axis=2, concat_axis=1, tiled=True)
    mats, width, cols = regrouped.shape
    rank = projectors.shape[2]
    projected = jnp.einsum(
        "dmr,mdc->mrc", projectors, regrouped, preferred_element_type=jnp.float32
    )
    first_new = 0.9 * first_moment.reshape(mats, rank, cols) + 0.1 * projected
    second_new = 0.999 * second_moment.reshape(mats, rank, cols) + 0.001 * projected * projected
    update = (first_new / CORR_FIRST / (jnp.sqrt(second_new / CORR_SECOND) + 1e-08)).astype(
        jnp.bfloat16
    )
    delta = jnp.einsum("dmr,mrc->mdc", projectors, update, preferred_element_type=jnp.float32)
    returned = lax.all_to_all(delta, "shard", split_axis=1, concat_axis=2, tiled=True)
    new_weight = weights - 0.2 * returned
    back = jnp.einsum(
        "mdc,dmr->mcr", regrouped, projectors, preferred_element_type=jnp.float32
    ).astype(jnp.bfloat16)
    partial_sum = jnp.einsum("mdc,mcr->dmr", regrouped, back, preferred_element_type=jnp.float32)
    refresh = lax.psum(partial_sum, ("shard", "tensor"))
    norms = jnp.sqrt(jnp.sum(refresh * refresh, axis=(0, 2)) + 1e-06)
    iterate = refresh / norms[None, :, None]
    for sweep in range(NS_STEPS):
        iterate = newton_steps(iterate, column_inner(iterate))
    new_basis = (iterate * factor).astype(jnp.bfloat16)
    shape_four = first_moment.shape
    return (new_weight, first_new.reshape(shape_four), second_new.reshape(shape_four), new_basis)


def solution(mesh):
    in_specs = (
        P(None, "shard", "tensor"),
        P(None, "shard", "tensor"),
        P(),
        P(None, None, "tensor", "shard"),
        P(None, None, "tensor", "shard"),
    )
    out_specs = (
        P(None, "shard", "tensor"),
        P(None, None, "tensor", "shard"),
        P(None, None, "tensor", "shard"),
        P(),
    )
    sizes = mesh.shape["shard"], mesh.shape["tensor"]
    body = functools.partial(per_device, *sizes) if sizes == (8, 4) else per_device_any
    return jax.shard_map(body, mesh=mesh, in_specs=in_specs, out_specs=out_specs, check_vma=False)
```

```python
import functools
import math

import jax
import jax.numpy as jnp
from jax import lax
from jax.experimental import pallas as pl
from jax.experimental.pallas import tpu as pltpu
from jax.sharding import PartitionSpec as P

NS_STEPS = 5
CORR_FIRST = 1.0
CORR_SECOND = 0.6323045752
HIGHEST = lax.Precision.HIGHEST
LANES = 128
VMEM = pl.BlockSpec(memory_space=pltpu.VMEM)
PARAMS = pltpu.CompilerParams(vmem_limit_bytes=32 * 1024 * 1024)


def dot(a, b, dims, **kw):
    return lax.dot_general(a, b, (dims, ((), ())), preferred_element_type=jnp.float32, **kw)


def nn(a, b, **kw):
    return dot(a, b, ((1,), (0,)), **kw)


def tn(a, b, **kw):
    return dot(a, b, ((0,), (0,)), **kw)


def nt(a, b, **kw):
    return dot(a, b, ((1,), (1,)), **kw)


def row_owner():
    tensor = lax.axis_index("tensor")
    return (tensor & 1) * 4 + (tensor >> 1) * 2 + (lax.axis_index("shard") & 1)


def fold_plan(rows, cols):
    tail = cols - LANES
    rest = 2 * tail - LANES
    stacked = -(-(rows // 2) // 16) * 8
    return tail, rest, stacked


def fold(block):
    rows, cols = block.shape
    tail, rest, stacked = fold_plan(rows, cols)
    half = rows // 2
    upper, lower = block[:half, LANES:], block[half:, LANES:]
    middle = jnp.concatenate([upper, lower[:, : tail - rest]], axis=1)
    left = lower[:, tail - rest :]
    below = jnp.concatenate(
        [left[stacked:], jnp.zeros((2 * stacked - half, rest), block.dtype)], axis=0
    )
    last = jnp.concatenate(
        [left[:stacked], below, jnp.zeros((stacked, LANES - 2 * rest), block.dtype)], axis=1
    )
    return jnp.concatenate([block[:, :LANES], middle, last], axis=0)


def unfold(folded, rows, cols):
    tail, rest, stacked = fold_plan(rows, cols)
    half = rows // 2
    middle, last = folded[rows : rows + half], folded[rows + half :]
    left = jnp.concatenate([last[:, :rest], last[: half - stacked, rest : 2 * rest]], axis=0)
    lower = jnp.concatenate([middle[:, tail:], left], axis=1)
    second = jnp.concatenate([middle[:, :tail], lower], axis=0)
    second = jnp.concatenate([second, jnp.zeros((rows, LANES - tail), folded.dtype)], axis=1)
    return jnp.concatenate([folded[:rows], second], axis=1)


def cut_kernel(parts, cols, groups, g_ref, *refs):
    outs, held = refs[:-1], refs[-1]
    size = held.shape[1]
    for part in range(parts):
        block = g_ref[0, :, part * cols : (part + 1) * cols].astype(jnp.float32)
        held[part] = fold(block).astype(held.dtype)
    me = lax.axis_index("shard")
    for out, group in zip(outs, groups):
        for i, k in enumerate(group):
            out[i * size : (i + 1) * size, :] = held[me ^ k]


def cut(gradients, mat, parts, cols, groups):
    _, rows, whole = gradients.shape
    size = folded_rows(rows, cols)
    shapes = [(len(group) * size, LANES) for group in groups]
    return pl.pallas_call(
        functools.partial(cut_kernel, parts, cols, groups),
        grid=(1,),
        in_specs=[pl.BlockSpec((1, rows, whole), lambda i: (mat, 0, 0))],
        out_specs=[pl.BlockSpec(shape, lambda i: (0, 0)) for shape in shapes],
        out_shape=[jax.ShapeDtypeStruct(shape, gradients.dtype) for shape in shapes],
        scratch_shapes=[pltpu.VMEM((parts, size, LANES), gradients.dtype)],
        compiler_params=PARAMS,
        name="cut_columns",
    )(gradients)


def folded_rows(rows, cols):
    return rows + rows // 2 + fold_plan(rows, cols)[2]


def pair_kernel(own_ref, got_ref, *outs):
    size = outs[0].shape[0] // 2
    for k, out in enumerate(outs):
        out[:size, :] = own_ref[k * size : (k + 1) * size, :]
        out[size:, :] = got_ref[k * size : (k + 1) * size, :]


def pair(own, got, count):
    size = own.shape[0] // count
    shape = (2 * size, LANES)
    return pl.pallas_call(
        pair_kernel,
        in_specs=[VMEM, VMEM],
        out_specs=[VMEM] * count,
        out_shape=[jax.ShapeDtypeStruct(shape, own.dtype)] * count,
        compiler_params=PARAMS,
        name="pair_blocks",
    )(own, got)


def project_kernel(rows, cols, inputs, each, *refs):
    blocks, (p_ref, first_ref, second_ref), refs = refs[:inputs], refs[inputs : inputs + 3], refs[inputs + 3 :]
    update_ref, first_out, second_out, send_ref, keep_ref, grad = refs[-6:]
    parts = inputs * each
    size = blocks[0].shape[0] // each
    me = lax.axis_index("shard")
    for k in range(parts):
        folded = blocks[k // each][(k % each) * size : (k % each + 1) * size, :]
        block = unfold(folded.astype(jnp.float32), rows, cols)
        grad[pl.ds(pl.multiple_of((me ^ k) * rows, rows), rows), :] = block.astype(grad.dtype)
    projected = tn(grad[...], p_ref[0])
    back = projected.astype(jnp.bfloat16)
    own = row_owner()
    half = parts // 2
    for j in list(range(half, parts)) + list(range(half)):
        at = pl.multiple_of((own ^ j) * rows, rows)
        term = nn(grad[pl.ds(at, rows), :], back)
        out = send_ref if j >= half else keep_ref
        out[(j % half) * rows : (j % half + 1) * rows, :] = term
    projected = projected[:cols]
    first_new = 0.9 * first_ref[0] + 0.1 * projected
    second_new = 0.999 * second_ref[0] + 0.001 * projected * projected
    first_out[0] = first_new
    second_out[0] = second_new
    update_ref[...] = (
        first_new / CORR_FIRST / (jnp.sqrt(second_new / CORR_SECOND) + 1e-08)
    ).astype(jnp.bfloat16)


def project(blocks, rows, projectors, first, second, mat, earlier):
    mats, width, rank = projectors.shape
    cols = first.shape[1]
    parts = width // rows
    inputs = len(blocks)
    wide = -(-cols // LANES) * LANES
    moment = pl.BlockSpec((1, cols, rank), lambda i: (mat, 0, 0))
    whole = lambda *shape: pl.BlockSpec(shape, lambda i: (0,) * len(shape))
    in_specs = [whole(*block.shape) for block in blocks]
    in_specs += [pl.BlockSpec((1, width, rank), lambda i: (mat, 0, 0)), moment, moment]
    in_specs += [pl.BlockSpec(memory_space=pl.ANY)] * len(earlier)
    half = width // 2
    return pl.pallas_call(
        functools.partial(project_kernel, rows, cols, inputs, parts // inputs),
        grid=(1,),
        in_specs=in_specs,
        out_specs=[whole(cols, rank), moment, moment, whole(half, rank), whole(half, rank)],
        out_shape=[
            jax.ShapeDtypeStruct((cols, rank), jnp.bfloat16),
            jax.ShapeDtypeStruct(first.shape, first.dtype),
            jax.ShapeDtypeStruct(second.shape, second.dtype),
            jax.ShapeDtypeStruct((half, rank), jnp.float32),
            jax.ShapeDtypeStruct((half, rank), jnp.float32),
        ],
        scratch_shapes=[pltpu.VMEM((width, wide), jnp.bfloat16)],
        input_output_aliases={inputs + 3 + i: 1 + i for i in range(len(earlier))},
        compiler_params=PARAMS,
        name="project",
    )(*blocks, projectors, first, second, *earlier)


def split(a):
    high = a.astype(jnp.bfloat16)
    return high, (a - high.astype(jnp.float32)).astype(jnp.bfloat16)


def product(a, b):
    return nn(a[0], b[0]) + (nn(a[0], b[1]) + nn(a[1], b[0]))


def basis_kernel(factor, low_ref, high_ref, *refs):
    out_ref = refs[-1]
    half, rank = low_ref.shape
    rows = half // 4
    low, high = low_ref[...], high_ref[...]
    square = jnp.sum(low * low) + jnp.sum(high * high) + 1e-06
    halves = split(low), split(high)
    cross = tn(halves[0][0], halves[0][1]) + tn(halves[1][0], halves[1][1])
    gram = tn(halves[0][0], halves[0][0]) + tn(halves[1][0], halves[1][0])
    gram = (gram + (cross + cross.T)) * (1.0 / square)
    eye = (
        lax.broadcasted_iota(jnp.int32, (rank, rank), 0)
        == lax.broadcasted_iota(jnp.int32, (rank, rank), 1)
    ).astype(jnp.float32)
    total = None
    for sweep in range(NS_STEPS):
        plain = 1.5 * eye - 0.5 * gram
        step = split(plain)
        if sweep < NS_STEPS - 1:
            gram = product(split(product(split(gram), step)), step)
        total = plain if total is None else product(split(total), step)
    total = split(total * (factor / jnp.sqrt(square)))
    own = row_owner()
    for j in range(8):
        span = slice((j % 4) * rows, (j % 4 + 1) * rows)
        block = product([part[span] for part in halves[j // 4]], total)
        at = pl.multiple_of((own ^ j) * rows, rows)
        out_ref[0, pl.ds(at, rows), :] = block.astype(jnp.bfloat16)


def basis(low, high, mat, mats, factor, earlier):
    half, rank = low.shape
    whole = lambda *shape: pl.BlockSpec(shape, lambda i: (0,) * len(shape))
    return pl.pallas_call(
        functools.partial(basis_kernel, factor),
        grid=(1,),
        in_specs=[whole(half, rank)] * 2 + [pl.BlockSpec(memory_space=pl.ANY)] * len(earlier),
        out_specs=pl.BlockSpec((1, 2 * half, rank), lambda i: (mat, 0, 0)),
        out_shape=jax.ShapeDtypeStruct((mats, 2 * half, rank), jnp.bfloat16),
        input_output_aliases={2: 0} if earlier else {},
        compiler_params=PARAMS,
        name="newton_schulz",
    )(low, high, *earlier)


def weight_kernel(cols, w_ref, p_ref, mine_ref, other_ref, *refs):
    out_ref, held = refs[-2:]
    rows = w_ref.shape[1]
    me = lax.axis_index("shard")
    z, x = me >> 1, me & 1
    early = z < 2
    order = [z, z ^ 1, jnp.where(early, 2, 1), jnp.where(early, 3, 0)]
    for i, place in enumerate(order):
        span = slice(i * cols, (i + 1) * cols)
        held[place * 2 + x] = mine_ref[span, :]
        held[place * 2 + (x ^ 1)] = other_ref[span, :]
    own = p_ref[0, pl.ds(pl.multiple_of(me * rows, rows), rows), :]
    for part in range(held.shape[0]):
        span = slice(part * cols, (part + 1) * cols)
        out_ref[0, :, span] = w_ref[0, :, span] - 0.2 * nt(own, held[part])


def weight_step(weights, projectors, mine, other, mat, earlier):
    mats, rows, whole = weights.shape
    _, width, rank = projectors.shape
    cols = mine.shape[0] // 4
    big = pl.BlockSpec((1, rows, whole), lambda i: (mat, 0, 0))
    flat = pl.BlockSpec(mine.shape, lambda i: (0, 0))
    return pl.pallas_call(
        functools.partial(weight_kernel, cols),
        grid=(1,),
        in_specs=[big, pl.BlockSpec((1, width, rank), lambda i: (mat, 0, 0)), flat, flat]
        + [pl.BlockSpec(memory_space=pl.ANY)] * len(earlier),
        out_specs=big,
        out_shape=jax.ShapeDtypeStruct(weights.shape, weights.dtype),
        scratch_shapes=[pltpu.VMEM((8, cols, rank), jnp.bfloat16)],
        input_output_aliases={4: 0} if earlier else {},
        compiler_params=PARAMS,
        name="weight_step",
    )(weights, projectors, mine, other, *earlier)


def swap(x, axis, size, bit):
    return lax.ppermute(x, axis, [(i, i ^ bit) for i in range(size)])


def spread(update):
    z = lax.axis_index("shard") >> 1
    near = swap(update, "shard", 8, 2)
    both = jnp.concatenate([update, near])
    middle = lax.ppermute(both, "shard", [(2, 4), (3, 5), (4, 2), (5, 3)])
    outer = lax.ppermute(middle, "shard", [(2, 0), (3, 1), (4, 6), (5, 7)])
    far = jnp.where((z == 1) | (z == 2), middle, outer)
    return jnp.concatenate([both, far])


def per_device(gradients, weights, projectors, first_moment, second_moment):
    factor = math.sqrt(projectors.shape[0])
    mats, rows, whole = gradients.shape
    cols = whole // 8
    across = jnp.swapaxes(projectors, 0, 1)
    first = jnp.swapaxes(first_moment[:, :, 0, :], 1, 2)
    second = jnp.swapaxes(second_moment[:, :, 0, :], 1, 2)
    core = lambda x: swap(x, "tensor", 4, 1)
    along_y = lambda x: swap(x, "tensor", 4, 2)
    along_x = lambda x: swap(x, "shard", 8, 1)
    z_far = lambda x: swap(x, "shard", 8, 4)
    z_near = lambda x: swap(x, "shard", 8, 2)

    def regroup(mat):
        if mat == 0:
            pieces = cut(gradients, mat, 8, cols, [(k,) for k in range(8)])
            return [pieces[0]] + [swap(pieces[k], "shard", 8, k) for k in range(1, 8)]
        own, sent = cut(gradients, mat, 8, cols, [(0, 2, 4, 6), (1, 3, 5, 7)])
        pieces = pair(own, along_x(sent), 4)
        return [pieces[0]] + [swap(pieces[k], "shard", 8, 2 * k) for k in range(1, 4)]

    blocks = [regroup(mat) for mat in range(mats)]
    moments, bases, new_weight, updates = (), (), (), []
    for mat in range(mats):
        update, *moments, send, keep = project(
            blocks[mat], rows, across, first, second, mat, moments
        )
        for exchange in (core, along_y, along_x):
            got = exchange(send)
            if keep.shape[0] > rows:
                half = keep.shape[0] // 2
                send, keep = keep[half:] + got[half:], keep[:half] + got[:half]
            else:
                keep = keep + got
        keep = keep + z_far(keep)
        keep = keep + z_near(keep)
        keep = jnp.concatenate([keep, along_x(keep)])
        keep = jnp.concatenate([keep, along_y(keep)])
        bases = (basis(keep, core(keep), mat, mats, factor, bases),)
        mine = spread(update)
        new_weight = (weight_step(weights, across, mine, along_x(mine), mat, new_weight),)
    back = lambda x: jnp.swapaxes(x, 1, 2)[:, :, None, :]
    return (new_weight[0], back(moments[0]), back(moments[1]), jnp.swapaxes(bases[0], 0, 1))


def newton_steps(iterate, inner):
    return 1.5 * iterate - 0.5 * jnp.einsum(
        "dmr,mrs->dms", iterate, inner, precision=HIGHEST, preferred_element_type=jnp.float32
    )


def column_inner(iterate):
    return jnp.einsum(
        "dmr,dms->mrs", iterate, iterate, precision=HIGHEST, preferred_element_type=jnp.float32
    )


def per_device_any(gradients, weights, projectors, first_moment, second_moment):
    factor = math.sqrt(projectors.shape[0])
    regrouped = lax.all_to_all(gradients, "shard", split_axis=2, concat_axis=1, tiled=True)
    mats, width, cols = regrouped.shape
    rank = projectors.shape[2]
    projected = jnp.einsum(
        "dmr,mdc->mrc", projectors, regrouped, preferred_element_type=jnp.float32
    )
    first_new = 0.9 * first_moment.reshape(mats, rank, cols) + 0.1 * projected
    second_new = 0.999 * second_moment.reshape(mats, rank, cols) + 0.001 * projected * projected
    update = (first_new / CORR_FIRST / (jnp.sqrt(second_new / CORR_SECOND) + 1e-08)).astype(
        jnp.bfloat16
    )
    delta = jnp.einsum("dmr,mrc->mdc", projectors, update, preferred_element_type=jnp.float32)
    returned = lax.all_to_all(delta, "shard", split_axis=1, concat_axis=2, tiled=True)
    new_weight = weights - 0.2 * returned
    back = jnp.einsum(
        "mdc,dmr->mcr", regrouped, projectors, preferred_element_type=jnp.float32
    ).astype(jnp.bfloat16)
    partial_sum = jnp.einsum("mdc,mcr->dmr", regrouped, back, preferred_element_type=jnp.float32)
    refresh = lax.psum(partial_sum, ("shard", "tensor"))
    norms = jnp.sqrt(jnp.sum(refresh * refresh, axis=(0, 2)) + 1e-06)
    iterate = refresh / norms[None, :, None]
    for sweep in range(NS_STEPS):
        iterate = newton_steps(iterate, column_inner(iterate))
    new_basis = (iterate * factor).astype(jnp.bfloat16)
    shape_four = first_moment.shape
    return (new_weight, first_new.reshape(shape_four), second_new.reshape(shape_four), new_basis)


def solution(mesh):
    in_specs = (
        P(None, "shard", "tensor"),
        P(None, "shard", "tensor"),
        P(),
        P(None, None, "tensor", "shard"),
        P(None, None, "tensor", "shard"),
    )
    out_specs = (
        P(None, "shard", "tensor"),
        P(None, None, "tensor", "shard"),
        P(None, None, "tensor", "shard"),
        P(),
    )
    own = (mesh.shape["shard"], mesh.shape["tensor"]) == (8, 4)
    body = per_device if own else per_device_any
    return jax.shard_map(body, mesh=mesh, in_specs=in_specs, out_specs=out_specs, check_vma=False)
```

```python
import functools
import math

import jax
import jax.numpy as jnp
from jax import lax
from jax.experimental import pallas as pl
from jax.experimental.pallas import tpu as pltpu
from jax.sharding import PartitionSpec as P

NS_STEPS = 5
CORR_FIRST = 1.0
CORR_SECOND = 0.6323045752
HIGHEST = lax.Precision.HIGHEST
LANES = 128
TOKEN = jax.ShapeDtypeStruct((8, 128), jnp.float32)
GROUPS = ((0, 1), (2,))
G_X = (False, False)
X_FIRST = (False, False)
Y_SPLIT = (False, False)
X_HIGH = (False, False)
Z_SPLIT = (False, False)
U_FAR = (False, False)
COST = {"newton_schulz": 10}
PLAN = (
    "cut:0",
    "cut:1",
    "project:0",
    "project:1",
    "core:0",
    "core:1",
    "join:0",
    "y:0",
    "wait:g03",
    "y:1",
    "x:0",
    "collect:0",
    "x:1",
    "far:0",
    "join:1",
    "far:1",
    "near:0",
    "near:1",
    "weight:1",
    "wait:un0",
    "collect:1",
    "weight:0",
    "basis:0",
    "basis:1",
    "weight:2",
)
PARAMS = pltpu.CompilerParams(vmem_limit_bytes=32 * 1024 * 1024)


def dot(a, b, dims, **kw):
    return lax.dot_general(a, b, (dims, ((), ())), preferred_element_type=jnp.float32, **kw)


def nn(a, b, **kw):
    return dot(a, b, ((1,), (0,)), **kw)


def tn(a, b, **kw):
    return dot(a, b, ((0,), (0,)), **kw)


def nt(a, b, **kw):
    return dot(a, b, ((1,), (1,)), **kw)


def block(shape, at=0):
    return pl.BlockSpec(shape, lambda i: (at,) + (0,) * (len(shape) - 1))


def call(
    kernel,
    inputs,
    in_specs,
    outs,
    out_specs=None,
    earlier=(),
    first_out=0,
    grid=1,
    after=(),
    scratch=(),
    name=None,
    us=0.5,
):
    in_specs = in_specs or [block(x.shape) for x in inputs]
    out_specs = out_specs or [block(x.shape) for x in outs]
    count, unused = len(inputs), len(earlier) + len(after)

    def body(*refs):
        kernel(*refs[:count], *refs[count + unused :])

    return pl.pallas_call(
        body,
        grid=(grid,),
        in_specs=in_specs + [pl.BlockSpec(memory_space=pl.ANY)] * unused,
        out_specs=out_specs,
        out_shape=outs,
        scratch_shapes=list(scratch),
        input_output_aliases={count + i: first_out + i for i in range(len(earlier))},
        compiler_params=PARAMS,
        cost_estimate=pl.CostEstimate(
            flops=int(us * COST.get(name, 5) * 1e9), bytes_accessed=int(us * COST.get(name, 5) * 3e6), transcendentals=0
        ),
        name=name,
    )(*inputs, *earlier, *after)


def row_owner(x_high):
    tensor = lax.axis_index("tensor")
    y, x = tensor >> 1, lax.axis_index("shard") & 1
    return (tensor & 1) * 4 + (x * 2 + y if x_high else y * 2 + x)


def fold_plan(rows, cols):
    tail = cols - LANES
    rest = 2 * tail - LANES
    stacked = -(-(rows // 2) // 16) * 8
    return tail, rest, stacked


def fold(block):
    rows, cols = block.shape
    tail, rest, stacked = fold_plan(rows, cols)
    half = rows // 2
    upper, lower = block[:half, LANES:], block[half:, LANES:]
    middle = jnp.concatenate([upper, lower[:, : tail - rest]], axis=1)
    left = lower[:, tail - rest :]
    below = jnp.concatenate(
        [left[stacked:], jnp.zeros((2 * stacked - half, rest), block.dtype)], axis=0
    )
    last = jnp.concatenate(
        [left[:stacked], below, jnp.zeros((stacked, LANES - 2 * rest), block.dtype)], axis=1
    )
    return jnp.concatenate([block[:, :LANES], middle, last], axis=0)


def unfold(folded, rows, cols):
    tail, rest, stacked = fold_plan(rows, cols)
    half = rows // 2
    middle, last = folded[rows : rows + half], folded[rows + half :]
    left = jnp.concatenate([last[:, :rest], last[: half - stacked, rest : 2 * rest]], axis=0)
    lower = jnp.concatenate([middle[:, tail:], left], axis=1)
    second = jnp.concatenate([middle[:, :tail], lower], axis=0)
    second = jnp.concatenate([second, jnp.zeros((rows, LANES - tail), folded.dtype)], axis=1)
    return jnp.concatenate([folded[:rows], second], axis=1)


def cut_kernel(cols, offsets, g_ref, *refs):
    outs, held = refs[:-1], refs[-1]
    parts, size, _ = held.shape
    for part in range(parts):
        columns = g_ref[0, :, part * cols : (part + 1) * cols].astype(jnp.float32)
        held[part] = fold(columns).astype(held.dtype)
    me = lax.axis_index("shard")
    for out, ks in zip(outs, offsets):
        for i, k in enumerate(ks):
            out[0, i * size : (i + 1) * size, :] = held[me ^ k]


def cut(gradients, group, parts, cols, offsets, after=()):
    _, rows, whole = gradients.shape
    size = folded_rows(rows, cols)
    return call(
        functools.partial(cut_kernel, cols, offsets),
        [gradients],
        [pl.BlockSpec((1, rows, whole), lambda i: (group[0] + i, 0, 0))],
        [
            jax.ShapeDtypeStruct((len(group), len(ks) * size, LANES), gradients.dtype)
            for ks in offsets
        ],
        out_specs=[
            pl.BlockSpec((1, len(ks) * size, LANES), lambda i: (i, 0, 0)) for ks in offsets
        ],
        grid=len(group),
        after=after,
        scratch=[pltpu.VMEM((parts, size, LANES), gradients.dtype)],
        name="cut_columns",
        us=len(group),
    )


def match_kernel(own_ref, got_ref, *outs):
    size = outs[0].shape[1] // 2
    for k, out in enumerate(outs):
        out[:, :size, :] = own_ref[:, k * size : (k + 1) * size, :]
        out[:, size:, :] = got_ref[:, k * size : (k + 1) * size, :]


def match(own, got, count, after=()):
    shape = jax.ShapeDtypeStruct((own.shape[0], own.shape[1] // count * 2, LANES), own.dtype)
    return call(match_kernel, [own, got], None, [shape] * count, after=after, name="match", us=0.7)


def folded_rows(rows, cols):
    return rows + rows // 2 + fold_plan(rows, cols)[2]


def project_kernel(offsets, x_high, rows, cols, *refs):
    count = len(offsets)
    parts = sum(len(ks) for ks in offsets)
    blocks, (p_ref, first_ref, second_ref), refs = refs[:count], refs[count : count + 3], refs[count + 3 :]
    update_ref, first_out, second_out, send_ref, keep_ref, grad = refs
    me = lax.axis_index("shard")
    size = folded_rows(rows, cols)
    for ref, ks in zip(blocks, offsets):
        for i, k in enumerate(ks):
            part = unfold(ref[0, i * size : (i + 1) * size, :].astype(jnp.float32), rows, cols)
            grad[pl.ds(pl.multiple_of((me ^ k) * rows, rows), rows), :] = part.astype(grad.dtype)
    projected = tn(grad[...], p_ref[0])
    back = projected.astype(jnp.bfloat16)
    own = row_owner(x_high)
    half = parts // 2
    for j in list(range(half, parts)) + list(range(half)):
        at = pl.multiple_of((own ^ j) * rows, rows)
        term = nn(grad[pl.ds(at, rows), :], back)
        out = send_ref if j >= half else keep_ref
        out[j % half, 0] = term
    projected = projected[:cols]
    first_new = 0.9 * first_ref[0] + 0.1 * projected
    second_new = 0.999 * second_ref[0] + 0.001 * projected * projected
    first_out[0] = first_new
    second_out[0] = second_new
    update_ref[0] = (
        first_new / CORR_FIRST / (jnp.sqrt(second_new / CORR_SECOND) + 1e-08)
    ).astype(jnp.bfloat16)


def project(blocks, offsets, x_high, group, rows, projectors, first, second, earlier, after=()):
    mats, width, rank = projectors.shape
    cols = first.shape[1]
    parts = sum(len(ks) for ks in offsets)
    count = len(group)
    wide = -(-cols // LANES) * LANES
    of_group = lambda *shape: pl.BlockSpec((1, *shape), lambda i: (group[0] + i, 0, 0))
    own = lambda *shape: pl.BlockSpec((1, *shape), lambda i: (i, 0, 0))
    half = pl.BlockSpec((parts // 2, 1, rows, rank), lambda i: (0, i, 0, 0))
    term = jax.ShapeDtypeStruct((parts // 2, count, rows, rank), jnp.float32)
    moment = of_group(cols, rank)
    return call(
        functools.partial(project_kernel, offsets, x_high, rows, cols),
        [*blocks, projectors, first, second],
        [own(*b.shape[1:]) for b in blocks] + [of_group(width, rank), moment, moment],
        [
            jax.ShapeDtypeStruct((count, cols, rank), jnp.bfloat16),
            jax.ShapeDtypeStruct(first.shape, first.dtype),
            jax.ShapeDtypeStruct(second.shape, second.dtype),
            term,
            term,
        ],
        out_specs=[own(cols, rank), moment, moment, half, half],
        grid=count,
        earlier=earlier,
        first_out=1,
        after=after,
        scratch=[pltpu.VMEM((width, wide), jnp.bfloat16)],
        name="project",
        us=2 * count,
    )


def sum_kernel(terms, inputs, *refs):
    ins, outs = refs[:inputs], refs[inputs:]
    for out, parts in zip(outs, terms):
        total = None
        for which, start in parts:
            value = ins[which][start : start + out.shape[0]]
            total = value if total is None else total + value
        out[...] = total


def sums(inputs, terms, after=()):
    shapes = [(count, *inputs[0].shape[1:]) for _, count in terms]
    return call(
        functools.partial(sum_kernel, [parts for parts, _ in terms], len(inputs)),
        inputs,
        None,
        [jax.ShapeDtypeStruct(shape, jnp.float32) for shape in shapes],
        after=after,
        name="sums",
        us=0.6,
    )


def halve_kernel(count, *refs):
    ins, outs = refs[:count], refs[count:]
    rows = outs[0].shape[2]
    for i, out in enumerate(outs):
        total = None
        for ref in ins:
            value = ref[:1, :, i * rows : (i + 1) * rows, :]
            total = value if total is None else total + value
        out[...] = total


def halve(inputs, after=()):
    _, count, rows, rank = inputs[0].shape
    shape = jax.ShapeDtypeStruct((1, count, rows // 2, rank), jnp.float32)
    return call(
        functools.partial(halve_kernel, len(inputs)),
        inputs,
        None,
        [shape] * 2,
        after=after,
        name="sums",
        us=0.6,
    )


def whole_kernel(a_ref, b_ref, c_ref, d_ref, out_ref):
    rows = a_ref.shape[2]
    out_ref[:, :, :rows, :] = a_ref[...] + b_ref[...]
    out_ref[:, :, rows:, :] = c_ref[...] + d_ref[...]


def whole(halves, got, after=()):
    _, count, rows, rank = halves[0].shape
    shape = jax.ShapeDtypeStruct((1, count, 2 * rows, rank), jnp.float32)
    ins = [halves[0], got[0], halves[1], got[1]]
    return call(whole_kernel, ins, None, [shape], after=after, name="sums", us=0.6)


def join_kernel(a_ref, b_ref, out_ref):
    count = a_ref.shape[0]
    out_ref[:count], out_ref[count:] = a_ref[...], b_ref[...]


def join(a, b, after=()):
    shape = jax.ShapeDtypeStruct((a.shape[0] + b.shape[0], *a.shape[1:]), a.dtype)
    return call(join_kernel, [a, b], None, [shape], after=after, name="join", us=0.4)


def collect_kernel(both_ref, middle_ref, outer_ref, out_ref):
    z = lax.axis_index("shard") >> 1
    inner = (z == 1) | (z == 2)
    out_ref[:2] = both_ref[...]

    @pl.when(inner)
    def _():
        out_ref[2:] = middle_ref[...]

    @pl.when(jnp.logical_not(inner))
    def _():
        out_ref[2:] = outer_ref[...]


def collect(both, middle, outer, after=()):
    shape = jax.ShapeDtypeStruct((4, *both.shape[1:]), both.dtype)
    return call(
        collect_kernel, [both, middle, outer], None, [shape], after=after, name="collect", us=0.6
    )


def split(a):
    high = a.astype(jnp.bfloat16)
    return high, (a - high.astype(jnp.float32)).astype(jnp.bfloat16)


def thrice(a, b):
    return nn(jnp.concatenate([a[0], a[0], a[1]], axis=1), jnp.concatenate([b[0], b[1], b[0]], axis=0))


def basis_kernel(factor, x_high, *refs):
    pieces, (out_ref, token_ref, held_high, held_low) = refs[:-4], refs[-4:]
    token_ref[...] = jnp.zeros_like(token_ref)
    count, width, rank = held_high.shape
    rows = width // 8
    eye = (
        lax.broadcasted_iota(jnp.int32, (rank, rank), 0)
        == lax.broadcasted_iota(jnp.int32, (rank, rank), 1)
    ).astype(jnp.float32)
    mats = range(count)
    square, grams = [], []
    for m in mats:
        total = 0.0
        for j, piece in enumerate(pieces):
            value = piece[0, m]
            total = total + jnp.sum(value * value)
            span = slice(j * rows, (j + 1) * rows)
            held_high[m, span, :], held_low[m, span, :] = split(value)
        square.append(total + 1e-06)
    for m in mats:
        high, low = held_high[m], held_low[m]
        both = tn(high, jnp.concatenate([high, low], axis=1))
        cross = both[:, rank:]
        grams.append((both[:, :rank] + (cross + cross.T)) * (1.0 / square[m]))
    totals = [None] * count
    for sweep in range(NS_STEPS):
        parts = [split(gram) for gram in grams]
        if sweep < NS_STEPS - 1:
            squares = [thrice(parts[m], parts[m]) for m in mats]
        if sweep == 0:
            totals = [1.5 * eye - 0.5 * gram for gram in grams]
        else:
            totals = [1.5 * totals[m] - 0.5 * thrice(split(totals[m]), parts[m]) for m in mats]
        if sweep < NS_STEPS - 1:
            cubes = [thrice(split(squares[m]), parts[m]) for m in mats]
            grams = [2.25 * grams[m] - 1.5 * squares[m] + 0.25 * cubes[m] for m in mats]
    own = row_owner(x_high)
    for m in mats:
        total = split(totals[m] * (factor / jnp.sqrt(square[m])))
        for j in range(8):
            span = slice(j * rows, (j + 1) * rows)
            value = thrice((held_high[m, span, :], held_low[m, span, :]), total)
            at = pl.multiple_of((own ^ j) * rows, rows)
            out_ref[m, pl.ds(at, rows), :] = value.astype(jnp.bfloat16)


def basis(pieces, x_high, group, mats, factor, earlier, after=()):
    _, count, rows, rank = pieces[0].shape
    width = 8 * rows
    span = pl.BlockSpec((count, width, rank), lambda i: (group[0] // count, 0, 0))
    return call(
        functools.partial(basis_kernel, factor, x_high),
        pieces,
        None,
        [jax.ShapeDtypeStruct((mats, width, rank), jnp.bfloat16), TOKEN],
        out_specs=[span, block(TOKEN.shape)],
        earlier=earlier,
        after=after,
        scratch=[pltpu.VMEM((count, width, rank), jnp.bfloat16)] * 2,
        name="newton_schulz",
        us=4 * count,
    )


def weight_kernel(cols, x_first, far, w_ref, p_ref, *refs):
    pieces, (out_ref, token_ref, held) = refs[:-3], refs[-3:]
    token_ref[...] = jnp.zeros_like(token_ref)
    rows = w_ref.shape[1]
    me = lax.axis_index("shard")
    z, x = me >> 1, me & 1
    early = z < 2
    order = [z, z ^ 1, jnp.where(early, 2, 1), jnp.where(early, 3, 0)]
    if far:
        order = [z, z ^ 1, z ^ 2, z ^ 3]
    if x_first:
        for i in range(4):
            place = x ^ (i % 2)
            held[order[i // 2] * 2 + place] = pieces[0][i, 0]
            if far:
                held[order[2 + i // 2] * 2 + place] = pieces[1][i, 0]
                continue
            inner = (z == 1) | (z == 2)

            @pl.when(inner)
            def _(i=i, place=place):
                held[order[2 + i // 2] * 2 + place] = pieces[1][i, 0]

            @pl.when(jnp.logical_not(inner))
            def _(i=i, place=place):
                held[order[2 + i // 2] * 2 + place] = pieces[2][i, 0]

    else:
        mine_ref, other_ref = pieces
        for i in range(4):
            held[order[i] * 2 + x] = mine_ref[i, 0]
            held[order[i] * 2 + (x ^ 1)] = other_ref[i, 0]
    own = p_ref[0, pl.ds(pl.multiple_of(me * rows, rows), rows), :]
    for part in range(held.shape[0]):
        span = slice(part * cols, (part + 1) * cols)
        out_ref[0, :, span] = w_ref[0, :, span] - 0.2 * nt(own, held[part])


def weight_step(weights, projectors, pieces, modes, place, mat, earlier, after=()):
    mats, rows, whole = weights.shape
    _, width, rank = projectors.shape
    cols = pieces[0].shape[2]
    part = pl.BlockSpec((4, 1, cols, rank), lambda i: (0, place, 0, 0))
    big = block((1, rows, whole), mat)
    return call(
        functools.partial(weight_kernel, cols, *modes),
        [weights, projectors, *pieces],
        [big, block((1, width, rank), mat)] + [part] * len(pieces),
        [jax.ShapeDtypeStruct(weights.shape, weights.dtype), TOKEN],
        out_specs=[big, block(TOKEN.shape)],
        earlier=earlier,
        after=after,
        scratch=[pltpu.VMEM((8, cols, rank), jnp.bfloat16)],
        name="weight_step",
        us=1.6,
    )


def swap(x, axis, size, bit):
    return lax.ppermute(x, axis, [(i, i ^ bit) for i in range(size)])


def core(x):
    return swap(x, "tensor", 4, 1)


def along_y(x):
    return swap(x, "tensor", 4, 2)


def along_x(x):
    return swap(x, "shard", 8, 1)


def z_near(x):
    return swap(x, "shard", 8, 2)


def z_far(x):
    return swap(x, "shard", 8, 4)


def z_middle(x):
    return lax.ppermute(x, "shard", [(2, 4), (3, 5), (4, 2), (5, 3)])


def z_outer(x):
    return lax.ppermute(x, "shard", [(2, 0), (3, 1), (4, 6), (5, 7)])


def per_device(gradients, weights, projectors, first_moment, second_moment):
    factor = math.sqrt(projectors.shape[0])
    mats, rows, across_tensor = gradients.shape
    cols = across_tensor // 8
    across = jnp.swapaxes(projectors, 0, 1)
    first = jnp.swapaxes(first_moment[:, :, 0, :], 1, 2)
    second = jnp.swapaxes(second_moment[:, :, 0, :], 1, 2)
    last, pending = [], []

    def after():
        found = (*last, *pending)
        pending.clear()
        return found

    def mark(outs):
        last[:] = [outs[0]]
        return outs

    moved = {}

    def move(name, way, x):
        moved[name] = way(x)
        return moved[name]

    def axes(g):
        return (along_x, along_y) if X_HIGH[g] else (along_y, along_x)

    groups, count = GROUPS, len(GROUPS)
    moments, bases, new_weight = (), (), ()
    update, state, send, spread = {}, {}, {}, {}
    blocks, offsets = {}, {}

    def by_offset(k):
        return lambda x: swap(x, "shard", 8, k)

    def step_cut(g):
        if G_X[g]:
            own, sent = mark(cut(gradients, groups[g], 8, cols, [(0, 2, 4, 6), (1, 3, 5, 7)], after()))
            blocks[g] = own, move(f"gx{g}", along_x, sent)
            return
        offsets[g] = [(k,) for k in range(8)]
        pieces = mark(cut(gradients, groups[g], 8, cols, offsets[g], after()))
        blocks[g] = [pieces[0]] + [move(f"g{g}{k}", by_offset(k), pieces[k]) for k in range(1, 8)]

    def step_match(g):
        offsets[g] = [(k, k + 1) for k in (0, 2, 4, 6)]
        pieces = mark(match(*blocks[g], 4, after()))
        blocks[g] = [pieces[0]] + [
            move(f"g{g}{k}", by_offset(2 * k), pieces[k]) for k in range(1, 4)
        ]

    def step_project(g):
        nonlocal moments
        update[g], *moments, sent, state[g] = mark(
            project(blocks[g], offsets[g], X_HIGH[g], groups[g], rows, across, first, second, moments, after())
        )
        send[g] = move(f"c{g}", core, sent)
        update[g] = update[g][None]
        if X_FIRST[g]:
            spread[g] = move(f"ux{g}", along_x, update[g])
        else:
            spread[g] = move(f"un{g}", z_near, update[g])

    def step_core(g):
        low, got = state[g], send[g]
        if not Y_SPLIT[g]:
            sent, state[g] = mark(
                sums([low, got], [([(0, 2), (1, 2)], 2), ([(0, 0), (1, 0)], 2)], after())
            )
            send[g] = (move(f"y{g}", axes(g)[0], sent),)
            return
        third, other, state[g] = mark(
            sums(
                [low, got],
                [([(0, 3), (1, 3)], 1), ([(0, 2), (1, 2)], 1), ([(0, 0), (1, 0)], 2)],
                after(),
            )
        )
        send[g] = move(f"y{g}", axes(g)[0], third), move(f"w{g}", axes(g)[0], other)

    def step_y(g):
        if not Y_SPLIT[g]:
            one, state[g] = mark(
                sums([state[g], *send[g]], [([(0, 1), (1, 1)], 1), ([(0, 0), (1, 0)], 1)], after())
            )
            send[g] = (move(f"x{g}", axes(g)[1], one),)
            return
        third, other = send[g]
        (one,) = mark(sums([state[g], third], [([(0, 1), (1, 0)], 1)], after()))
        send[g] = other, move(f"x{g}", axes(g)[1], one)

    def step_x(g):
        adds = [state[g], *send[g]]
        if Z_SPLIT[g]:
            state[g] = mark(halve(adds, after()))
            send[g] = move(f"f{g}", z_far, state[g][0]), move(f"p{g}", z_near, state[g][1])
            return
        (state[g],) = mark(sums(adds, [([(i, 0) for i in range(len(adds))], 1)], after()))
        send[g] = move(f"f{g}", z_far, state[g])

    def step_far(g):
        if Z_SPLIT[g]:
            inputs = [state[g][0], send[g][0], state[g][1], send[g][1]]
            state[g] = mark(sums(inputs, [([(0, 0), (1, 0)], 1), ([(2, 0), (3, 0)], 1)], after()))
            send[g] = move(f"n{g}", z_near, state[g][0]), move(f"q{g}", z_far, state[g][1])
            return
        (state[g],) = mark(sums([state[g], send[g]], [([(0, 0), (1, 0)], 1)], after()))
        send[g] = move(f"n{g}", z_near, state[g])

    def step_near(g):
        if Z_SPLIT[g]:
            (a,) = mark(whole(state[g], send[g], after()))
        else:
            (a,) = mark(sums([state[g], send[g]], [([(0, 0), (1, 0)], 1)], after()))
        first_way, second_way = axes(g)
        b = move(f"X{g}", second_way, a)
        low = [a, b, move(f"Y{g}", first_way, a), move(f"W{g}", first_way, b)]
        state[g] = low + [move(f"C{g}{i}", core, piece) for i, piece in enumerate(low)]

    def step_pair(g):
        update[g] = mark(join(update[g], spread[g], after()))[0]
        spread[g] = move(f"un{g}", z_near, update[g])

    def step_join(g):
        (both,) = mark(join(update[g], spread[g], after()))
        if U_FAR[g]:
            spread[g] = both, move(f"um{g}", z_far, both)
            return
        middle = move(f"um{g}", z_middle, both)
        spread[g] = both, middle, move(f"uo{g}", z_outer, middle)

    def step_collect(g):
        gather = join if U_FAR[g] else collect
        (mine,) = mark(gather(*spread[g], after()))
        spread[g] = mine, move(f"ux{g}", along_x, mine)

    def step_weight(mat):
        nonlocal new_weight
        g = [mat in group for group in groups].index(True)
        place = groups[g].index(mat)
        *new_weight, token = weight_step(
            weights, across, spread[g], (X_FIRST[g], U_FAR[g]), place, mat, new_weight, after()
        )
        mark([token])

    def step_basis(g):
        nonlocal bases
        *bases, token = basis(state[g], X_HIGH[g], groups[g], mats, factor, bases, after())
        mark([token])

    steps = {
        "cut": step_cut,
        "match": step_match,
        "project": step_project,
        "core": step_core,
        "y": step_y,
        "x": step_x,
        "far": step_far,
        "near": step_near,
        "pair": step_pair,
        "join": step_join,
        "collect": step_collect,
        "weight": step_weight,
        "basis": step_basis,
    }
    for entry in PLAN:
        name, which = entry.split(":")
        if name == "wait":
            pending.append(moved[which])
        else:
            steps[name](int(which))
    back = lambda x: jnp.swapaxes(x, 1, 2)[:, :, None, :]
    return (new_weight[0], back(moments[0]), back(moments[1]), jnp.swapaxes(bases[0], 0, 1))


def newton_steps(iterate, inner):
    return 1.5 * iterate - 0.5 * jnp.einsum(
        "dmr,mrs->dms", iterate, inner, precision=HIGHEST, preferred_element_type=jnp.float32
    )


def column_inner(iterate):
    return jnp.einsum(
        "dmr,dms->mrs", iterate, iterate, precision=HIGHEST, preferred_element_type=jnp.float32
    )


def per_device_any(gradients, weights, projectors, first_moment, second_moment):
    factor = math.sqrt(projectors.shape[0])
    regrouped = lax.all_to_all(gradients, "shard", split_axis=2, concat_axis=1, tiled=True)
    mats, width, cols = regrouped.shape
    rank = projectors.shape[2]
    projected = jnp.einsum(
        "dmr,mdc->mrc", projectors, regrouped, preferred_element_type=jnp.float32
    )
    first_new = 0.9 * first_moment.reshape(mats, rank, cols) + 0.1 * projected
    second_new = 0.999 * second_moment.reshape(mats, rank, cols) + 0.001 * projected * projected
    update = (first_new / CORR_FIRST / (jnp.sqrt(second_new / CORR_SECOND) + 1e-08)).astype(
        jnp.bfloat16
    )
    delta = jnp.einsum("dmr,mrc->mdc", projectors, update, preferred_element_type=jnp.float32)
    returned = lax.all_to_all(delta, "shard", split_axis=1, concat_axis=2, tiled=True)
    new_weight = weights - 0.2 * returned
    back = jnp.einsum(
        "mdc,dmr->mcr", regrouped, projectors, preferred_element_type=jnp.float32
    ).astype(jnp.bfloat16)
    partial_sum = jnp.einsum("mdc,mcr->dmr", regrouped, back, preferred_element_type=jnp.float32)
    refresh = lax.psum(partial_sum, ("shard", "tensor"))
    norms = jnp.sqrt(jnp.sum(refresh * refresh, axis=(0, 2)) + 1e-06)
    iterate = refresh / norms[None, :, None]
    for sweep in range(NS_STEPS):
        iterate = newton_steps(iterate, column_inner(iterate))
    new_basis = (iterate * factor).astype(jnp.bfloat16)
    shape_four = first_moment.shape
    return (new_weight, first_new.reshape(shape_four), second_new.reshape(shape_four), new_basis)


def solution(mesh):
    in_specs = (
        P(None, "shard", "tensor"),
        P(None, "shard", "tensor"),
        P(),
        P(None, None, "tensor", "shard"),
        P(None, None, "tensor", "shard"),
    )
    out_specs = (
        P(None, "shard", "tensor"),
        P(None, None, "tensor", "shard"),
        P(None, None, "tensor", "shard"),
        P(),
    )
    own = (mesh.shape["shard"], mesh.shape["tensor"]) == (8, 4)
    body = per_device if own else per_device_any
    return jax.shard_map(body, mesh=mesh, in_specs=in_specs, out_specs=out_specs, check_vma=False)
```

```python
import functools
import math

import jax
import jax.numpy as jnp
from jax import lax
from jax.experimental import pallas as pl
from jax.experimental.pallas import tpu as pltpu
from jax.sharding import PartitionSpec as P

NS_STEPS = 5
CORR_FIRST = 1.0
CORR_SECOND = 0.6323045752
HIGHEST = lax.Precision.HIGHEST
LANES = 128
TOKEN = jax.ShapeDtypeStruct((8, 128), jnp.float32)
GROUPS = ((0, 1), (2,))
G_X = (False, False)
X_FIRST = (False, True)
X_HIGH = (False, True)
Z_NEAR = (False, False)
U_FAR = (False, False)
JOIN_BACK = (False, False)
CUT_LIMIT = 32
COST = {"newton_schulz": 10}
PLAN = (
    "cut:0",
    "cut:1",
    "project:0",
    "project:1",
    "core:0",
    "core:1",
    "pair:1",
    "join:0",
    "y:0",
    "y:1",
    "x:0",
    "x:1",
    "collect:0",
    "far:0",
    "join:1",
    "far:1",
    "near:0",
    "near:1",
    "weight:1",
    "weight:0",
    "weight:2",
    "basis:9",
)
def dot(a, b, dims, **kw):
    return lax.dot_general(a, b, (dims, ((), ())), preferred_element_type=jnp.float32, **kw)


def nn(a, b, **kw):
    return dot(a, b, ((1,), (0,)), **kw)


def tn(a, b, **kw):
    return dot(a, b, ((0,), (0,)), **kw)


def nt(a, b, **kw):
    return dot(a, b, ((1,), (1,)), **kw)


def block(shape, at=0):
    return pl.BlockSpec(shape, lambda i: (at,) + (0,) * (len(shape) - 1))


def call(
    kernel,
    inputs,
    in_specs,
    outs,
    out_specs=None,
    earlier=(),
    first_out=0,
    grid=1,
    after=(),
    scratch=(),
    name=None,
    us=0.5,
    limit=32,
):
    in_specs = in_specs or [block(x.shape) for x in inputs]
    out_specs = out_specs or [block(x.shape) for x in outs]
    count, unused = len(inputs), len(earlier) + len(after)

    def body(*refs):
        kernel(*refs[:count], *refs[count + unused :])

    return pl.pallas_call(
        body,
        grid=(grid,),
        in_specs=in_specs + [pl.BlockSpec(memory_space=pl.ANY)] * unused,
        out_specs=out_specs,
        out_shape=outs,
        scratch_shapes=list(scratch),
        input_output_aliases={count + i: first_out + i for i in range(len(earlier))},
        compiler_params=pltpu.CompilerParams(vmem_limit_bytes=limit * 1024 * 1024),
        cost_estimate=pl.CostEstimate(
            flops=int(us * COST.get(name, 5) * 1e9), bytes_accessed=int(us * COST.get(name, 5) * 3e6), transcendentals=0
        ),
        name=name,
    )(*inputs, *earlier, *after)


def row_owner(x_high):
    tensor = lax.axis_index("tensor")
    y, x = tensor >> 1, lax.axis_index("shard") & 1
    return (tensor & 1) * 4 + (x * 2 + y if x_high else y * 2 + x)


def fold_plan(rows, cols):
    tail = cols - LANES
    rest = 2 * tail - LANES
    stacked = -(-(rows // 2) // 16) * 8
    return tail, rest, stacked


def fold(block):
    rows, cols = block.shape
    tail, rest, stacked = fold_plan(rows, cols)
    half = rows // 2
    upper, lower = block[:half, LANES:], block[half:, LANES:]
    middle = jnp.concatenate([upper, lower[:, : tail - rest]], axis=1)
    left = lower[:, tail - rest :]
    below = jnp.concatenate(
        [left[stacked:], jnp.zeros((2 * stacked - half, rest), block.dtype)], axis=0
    )
    last = jnp.concatenate(
        [left[:stacked], below, jnp.zeros((stacked, LANES - 2 * rest), block.dtype)], axis=1
    )
    return jnp.concatenate([block[:, :LANES], middle, last], axis=0)


def unfold(folded, rows, cols):
    tail, rest, stacked = fold_plan(rows, cols)
    half = rows // 2
    middle, last = folded[rows : rows + half], folded[rows + half :]
    left = jnp.concatenate([last[:, :rest], last[: half - stacked, rest : 2 * rest]], axis=0)
    lower = jnp.concatenate([middle[:, tail:], left], axis=1)
    second = jnp.concatenate([middle[:, :tail], lower], axis=0)
    second = jnp.concatenate([second, jnp.zeros((rows, LANES - tail), folded.dtype)], axis=1)
    return jnp.concatenate([folded[:rows], second], axis=1)


def cut_kernel(cols, offsets, g_ref, *refs):
    outs, held = refs[:-1], refs[-1]
    parts, size, _ = held.shape
    for part in range(parts):
        columns = g_ref[0, :, part * cols : (part + 1) * cols].astype(jnp.float32)
        held[part] = fold(columns).astype(held.dtype)
    me = lax.axis_index("shard")
    for out, ks in zip(outs, offsets):
        for i, k in enumerate(ks):
            out[0, i * size : (i + 1) * size, :] = held[me ^ k]


def cut(gradients, group, parts, cols, offsets, after=()):
    _, rows, whole = gradients.shape
    size = folded_rows(rows, cols)
    return call(
        functools.partial(cut_kernel, cols, offsets),
        [gradients],
        [pl.BlockSpec((1, rows, whole), lambda i: (group[0] + i, 0, 0))],
        [
            jax.ShapeDtypeStruct((len(group), len(ks) * size, LANES), gradients.dtype)
            for ks in offsets
        ],
        out_specs=[
            pl.BlockSpec((1, len(ks) * size, LANES), lambda i: (i, 0, 0)) for ks in offsets
        ],
        grid=len(group),
        after=after,
        scratch=[pltpu.VMEM((parts, size, LANES), gradients.dtype)],
        name="cut_columns",
        us=len(group),
        limit=CUT_LIMIT,
    )


def match_kernel(own_ref, got_ref, *outs):
    size = outs[0].shape[1] // 2
    for k, out in enumerate(outs):
        out[:, :size, :] = own_ref[:, k * size : (k + 1) * size, :]
        out[:, size:, :] = got_ref[:, k * size : (k + 1) * size, :]


def match(own, got, count, after=()):
    shape = jax.ShapeDtypeStruct((own.shape[0], own.shape[1] // count * 2, LANES), own.dtype)
    return call(match_kernel, [own, got], None, [shape] * count, after=after, name="match", us=0.7)


def folded_rows(rows, cols):
    return rows + rows // 2 + fold_plan(rows, cols)[2]


def project_kernel(offsets, highs, rows, cols, *refs):
    count = len(offsets)
    parts = sum(len(ks) for ks in offsets)
    blocks, (p_ref, first_ref, second_ref), refs = refs[:count], refs[count : count + 3], refs[count + 3 :]
    update_ref, first_out, second_out, *terms, grad = refs
    me = lax.axis_index("shard")
    size = folded_rows(rows, cols)
    for ref, ks in zip(blocks, offsets):
        for i, k in enumerate(ks):
            part = unfold(ref[0, i * size : (i + 1) * size, :].astype(jnp.float32), rows, cols)
            grad[pl.ds(pl.multiple_of((me ^ k) * rows, rows), rows), :] = part.astype(grad.dtype)
    projected = tn(grad[...], p_ref[0])
    back = projected.astype(jnp.bfloat16)
    half = parts // 2
    for h, x_high in enumerate(highs):
        own = row_owner(x_high)
        columns = back[:, h * LANES : (h + 1) * LANES]
        for j in range(parts):
            at = pl.multiple_of((own ^ j) * rows, rows)
            terms[2 * h + j // half][j % half, 0] = nn(grad[pl.ds(at, rows), :], columns)
    projected = projected[:cols]
    first_new = 0.9 * first_ref[0] + 0.1 * projected
    second_new = 0.999 * second_ref[0] + 0.001 * projected * projected
    first_out[0] = first_new
    second_out[0] = second_new
    update_ref[0] = (
        first_new / CORR_FIRST / (jnp.sqrt(second_new / CORR_SECOND) + 1e-08)
    ).astype(jnp.bfloat16)


def project(blocks, offsets, highs, group, rows, projectors, first, second, earlier, after=()):
    mats, width, rank = projectors.shape
    cols = first.shape[1]
    parts = sum(len(ks) for ks in offsets)
    count = len(group)
    wide = -(-cols // LANES) * LANES
    of_group = lambda *shape: pl.BlockSpec((1, *shape), lambda i: (group[0] + i, 0, 0))
    own = lambda *shape: pl.BlockSpec((1, *shape), lambda i: (i, 0, 0))
    half = pl.BlockSpec((parts // 2, 1, rows, LANES), lambda i: (0, i, 0, 0))
    term = jax.ShapeDtypeStruct((parts // 2, count, rows, LANES), jnp.float32)
    number = 2 * len(highs)
    moment = of_group(cols, rank)
    return call(
        functools.partial(project_kernel, offsets, highs, rows, cols),
        [*blocks, projectors, first, second],
        [own(*b.shape[1:]) for b in blocks] + [of_group(width, rank), moment, moment],
        [
            jax.ShapeDtypeStruct((count, cols, rank), jnp.bfloat16),
            jax.ShapeDtypeStruct(first.shape, first.dtype),
            jax.ShapeDtypeStruct(second.shape, second.dtype),
        ]
        + [term] * number,
        out_specs=[own(cols, rank), moment, moment] + [half] * number,
        grid=count,
        earlier=earlier,
        first_out=1,
        after=after,
        scratch=[pltpu.VMEM((width, wide), jnp.bfloat16)],
        name="project",
        us=2 * count,
    )


def sum_kernel(terms, inputs, *refs):
    ins, outs = refs[:inputs], refs[inputs:]
    for out, parts in zip(outs, terms):
        total = None
        for which, start in parts:
            value = ins[which][start : start + out.shape[0]]
            total = value if total is None else total + value
        out[...] = total


def sums(inputs, terms, after=()):
    shapes = [(count, *inputs[0].shape[1:]) for _, count in terms]
    return call(
        functools.partial(sum_kernel, [parts for parts, _ in terms], len(inputs)),
        inputs,
        None,
        [jax.ShapeDtypeStruct(shape, jnp.float32) for shape in shapes],
        after=after,
        name="sums",
        us=0.6,
    )


def merge_kernel(count, *refs):
    ins, (sent_ref, low_ref) = refs[: 2 * count], refs[2 * count :]
    half = sent_ref.shape[0]
    at = 0
    for keep, got in zip(ins[:count], ins[count:]):
        span = slice(at, at + keep.shape[1])
        low_ref[:, span] = keep[:half] + got[:half]
        sent_ref[:, span] = keep[half:] + got[half:]
        at += keep.shape[1]


def merge(keeps, gots, after=()):
    blocks, _, rows, lanes = keeps[0].shape
    mats = sum(keep.shape[1] for keep in keeps)
    shape = jax.ShapeDtypeStruct((blocks // 2, mats, rows, lanes), jnp.float32)
    return call(
        functools.partial(merge_kernel, len(keeps)),
        [*keeps, *gots],
        None,
        [shape] * 2,
        after=after,
        name="sums",
        us=0.6,
    )


def hold_kernel(in_ref, out_ref):
    out_ref[...] = in_ref[...]


def hold(x, after=()):
    shape = jax.ShapeDtypeStruct(x.shape, x.dtype)
    return call(hold_kernel, [x], None, [shape], after=after, name="join", us=0.3)


def join_kernel(a_ref, b_ref, out_ref):
    count = a_ref.shape[0]
    out_ref[:count], out_ref[count:] = a_ref[...], b_ref[...]


def join(a, b, after=()):
    shape = jax.ShapeDtypeStruct((a.shape[0] + b.shape[0], *a.shape[1:]), a.dtype)
    return call(join_kernel, [a, b], None, [shape], after=after, name="join", us=0.4)


def collect_kernel(both_ref, middle_ref, outer_ref, out_ref):
    z = lax.axis_index("shard") >> 1
    inner = (z == 1) | (z == 2)
    out_ref[:2] = both_ref[...]

    @pl.when(inner)
    def _():
        out_ref[2:] = middle_ref[...]

    @pl.when(jnp.logical_not(inner))
    def _():
        out_ref[2:] = outer_ref[...]


def collect(both, middle, outer, after=()):
    shape = jax.ShapeDtypeStruct((4, *both.shape[1:]), both.dtype)
    return call(
        collect_kernel, [both, middle, outer], None, [shape], after=after, name="collect", us=0.6
    )


def split(a):
    high = a.astype(jnp.bfloat16)
    return high, (a - high.astype(jnp.float32)).astype(jnp.bfloat16)


def thrice(a, b):
    return nn(jnp.concatenate([a[0], a[0], a[1]], axis=1), jnp.concatenate([b[0], b[1], b[0]], axis=0))


def basis_kernel(factor, highs, *refs):
    refs, (out_ref, token_ref, held_high, held_low) = refs[:-4], refs[-4:]
    token_ref[...] = jnp.zeros_like(token_ref)
    count, width, rank = held_high.shape
    rows = width // 8
    mats = range(count)
    square, grams = [0.0] * count, []
    first = 0
    for h, (x_high, number) in enumerate(highs):
        half = refs[first : first + number]
        first += number
        own = row_owner(x_high)
        lanes = slice(h * LANES, (h + 1) * LANES)
        for j, (ref, i) in enumerate([(ref, i) for ref in half for i in range(ref.shape[0])]):
            at = pl.multiple_of((own ^ j) * rows, rows)
            for m in mats:
                value = ref[i, m]
                square[m] = square[m] + jnp.sum(value * value)
                high, low = split(value)
                held_high[m, pl.ds(at, rows), lanes] = high
                held_low[m, pl.ds(at, rows), lanes] = low
    square = [total + 1e-06 for total in square]
    eye = (
        lax.broadcasted_iota(jnp.int32, (rank, rank), 0)
        == lax.broadcasted_iota(jnp.int32, (rank, rank), 1)
    ).astype(jnp.float32)
    for m in mats:
        high, low = held_high[m], held_low[m]
        both = tn(high, jnp.concatenate([high, low], axis=1))
        cross = both[:, rank:]
        grams.append((both[:, :rank] + (cross + cross.T)) * (1.0 / square[m]))
    totals = [None] * count
    for sweep in range(NS_STEPS):
        parts = [split(gram) for gram in grams]
        if sweep < NS_STEPS - 1:
            squares = [thrice(parts[m], parts[m]) for m in mats]
        if sweep == 0:
            totals = [1.5 * eye - 0.5 * gram for gram in grams]
        else:
            totals = [1.5 * totals[m] - 0.5 * thrice(split(totals[m]), parts[m]) for m in mats]
        if sweep < NS_STEPS - 1:
            cubes = [thrice(split(squares[m]), parts[m]) for m in mats]
            grams = [2.25 * grams[m] - 1.5 * squares[m] + 0.25 * cubes[m] for m in mats]
    for m in mats:
        total = split(totals[m] * (factor / jnp.sqrt(square[m])))
        for j in range(8):
            span = slice(j * rows, (j + 1) * rows)
            value = thrice((held_high[m, span, :], held_low[m, span, :]), total)
            out_ref[m, span, :] = value.astype(jnp.bfloat16)


def basis(pieces, highs, rank, factor, after=()):
    _, count, rows, _ = pieces[0].shape
    width = 8 * rows
    return call(
        functools.partial(basis_kernel, factor, highs),
        pieces,
        None,
        [jax.ShapeDtypeStruct((count, width, rank), jnp.bfloat16), TOKEN],
        after=after,
        scratch=[pltpu.VMEM((count, width, rank), jnp.bfloat16)] * 2,
        name="newton_schulz",
        us=8,
    )


def weight_kernel(cols, x_first, far, w_ref, p_ref, *refs):
    pieces, (out_ref, token_ref, held) = refs[:-3], refs[-3:]
    token_ref[...] = jnp.zeros_like(token_ref)
    rows = w_ref.shape[1]
    me = lax.axis_index("shard")
    z, x = me >> 1, me & 1
    early = z < 2
    order = [z, z ^ 1, jnp.where(early, 2, 1), jnp.where(early, 3, 0)]
    if far:
        order = [z, z ^ 1, z ^ 2, z ^ 3]
    if x_first:
        for i in range(4):
            place = x ^ (i % 2)
            held[order[i // 2] * 2 + place] = pieces[0][i, 0]
            if far:
                held[order[2 + i // 2] * 2 + place] = pieces[1][i, 0]
                continue
            inner = (z == 1) | (z == 2)

            @pl.when(inner)
            def _(i=i, place=place):
                held[order[2 + i // 2] * 2 + place] = pieces[1][i, 0]

            @pl.when(jnp.logical_not(inner))
            def _(i=i, place=place):
                held[order[2 + i // 2] * 2 + place] = pieces[2][i, 0]

    else:
        mine_ref, other_ref = pieces
        for i in range(4):
            held[order[i] * 2 + x] = mine_ref[i, 0]
            held[order[i] * 2 + (x ^ 1)] = other_ref[i, 0]
    own = p_ref[0, pl.ds(pl.multiple_of(me * rows, rows), rows), :]
    for part in range(held.shape[0]):
        span = slice(part * cols, (part + 1) * cols)
        out_ref[0, :, span] = w_ref[0, :, span] - 0.2 * nt(own, held[part])


def weight_step(weights, projectors, pieces, modes, place, mat, earlier, after=()):
    mats, rows, whole = weights.shape
    _, width, rank = projectors.shape
    cols = pieces[0].shape[2]
    part = pl.BlockSpec((4, 1, cols, rank), lambda i: (0, place, 0, 0))
    big = block((1, rows, whole), mat)
    return call(
        functools.partial(weight_kernel, cols, *modes),
        [weights, projectors, *pieces],
        [big, block((1, width, rank), mat)] + [part] * len(pieces),
        [jax.ShapeDtypeStruct(weights.shape, weights.dtype), TOKEN],
        out_specs=[big, block(TOKEN.shape)],
        earlier=earlier,
        after=after,
        scratch=[pltpu.VMEM((8, cols, rank), jnp.bfloat16)],
        name="weight_step",
        us=1.6,
    )


def swap(x, axis, size, bit):
    return lax.ppermute(x, axis, [(i, i ^ bit) for i in range(size)])


def core(x):
    return swap(x, "tensor", 4, 1)


def along_y(x):
    return swap(x, "tensor", 4, 2)


def along_x(x):
    return swap(x, "shard", 8, 1)


def z_near(x):
    return swap(x, "shard", 8, 2)


def z_far(x):
    return swap(x, "shard", 8, 4)


def z_middle(x):
    return lax.ppermute(x, "shard", [(2, 4), (3, 5), (4, 2), (5, 3)])


def z_outer(x):
    return lax.ppermute(x, "shard", [(2, 0), (3, 1), (4, 6), (5, 7)])


def per_device(gradients, weights, projectors, first_moment, second_moment):
    factor = math.sqrt(projectors.shape[0])
    mats, rows, across_tensor = gradients.shape
    cols = across_tensor // 8
    across = jnp.swapaxes(projectors, 0, 1)
    first = jnp.swapaxes(first_moment[:, :, 0, :], 1, 2)
    second = jnp.swapaxes(second_moment[:, :, 0, :], 1, 2)
    last, pending = [], []

    def after():
        found = (*last, *pending)
        pending.clear()
        return found

    def mark(outs):
        last[:] = [outs[0]]
        return outs

    moved = {}

    def move(name, way, x):
        moved[name] = way(x)
        return moved[name]

    def axes(g):
        return (along_x, along_y) if X_HIGH[g] else (along_y, along_x)

    groups, count = GROUPS, len(GROUPS)
    moments, bases, new_weight = (), (), ()
    update, state, send, spread, kept, sent = {}, {}, {}, {}, {}, {}
    blocks, offsets = {}, {}

    def by_offset(k):
        return lambda x: swap(x, "shard", 8, k)

    def step_cut(g):
        if G_X[g]:
            own, sent = mark(cut(gradients, groups[g], 8, cols, [(0, 2, 4, 6), (1, 3, 5, 7)], after()))
            blocks[g] = own, move(f"gx{g}", along_x, sent)
            return
        offsets[g] = [(k,) for k in range(8)]
        pieces = mark(cut(gradients, groups[g], 8, cols, offsets[g], after()))
        blocks[g] = [pieces[0]] + [move(f"g{g}{k}", by_offset(k), pieces[k]) for k in range(1, 8)]

    def step_match(g):
        offsets[g] = [(k, k + 1) for k in (0, 2, 4, 6)]
        pieces = mark(match(*blocks[g], 4, after()))
        blocks[g] = [pieces[0]] + [
            move(f"g{g}{k}", by_offset(2 * k), pieces[k]) for k in range(1, 4)
        ]

    def step_project(g):
        nonlocal moments
        update[g], first_new, second_new, *terms = mark(
            project(
                blocks[g], offsets[g], X_HIGH, groups[g], rows, across, first, second, moments, after()
            )
        )
        moments = first_new, second_new
        kept[g] = terms[0::2]
        sent[g] = [move(f"c{g}{h}", core, term) for h, term in enumerate(terms[1::2])]
        update[g] = update[g][None]
        if X_FIRST[g]:
            spread[g] = move(f"ux{g}", along_x, update[g])
        elif f"un:{g}" not in PLAN:
            spread[g] = move(f"un{g}", z_near, update[g])

    def step_un(g):
        (update[g],) = mark(hold(update[g], after()))
        spread[g] = move(f"un{g}", z_near, update[g])


    def step_core(h):
        upper, state[h] = mark(
            merge([kept[g][h] for g in range(count)], [sent[g][h] for g in range(count)], after())
        )
        send[h] = move(f"y{h}", axes(h)[0], upper)

    def step_y(h):
        one, state[h] = mark(
            sums([state[h], send[h]], [([(0, 1), (1, 1)], 1), ([(0, 0), (1, 0)], 1)], after())
        )
        send[h] = move(f"x{h}", axes(h)[1], one)

    def step_x(h):
        (state[h],) = mark(sums([state[h], send[h]], [([(0, 0), (1, 0)], 1)], after()))
        send[h] = move(f"f{h}", z_near if Z_NEAR[h] else z_far, state[h])

    def step_far(h):
        (state[h],) = mark(sums([state[h], send[h]], [([(0, 0), (1, 0)], 1)], after()))
        send[h] = move(f"n{h}", z_far if Z_NEAR[h] else z_near, state[h])

    def step_near(h):
        (a,) = mark(sums([state[h], send[h]], [([(0, 0), (1, 0)], 1)], after()))
        first_way, second_way = axes(h)
        b = move(f"X{h}", second_way, a)
        if JOIN_BACK[h]:
            state[h] = a, b
            return
        low = [a, b, move(f"Y{h}", first_way, a), move(f"W{h}", first_way, b)]
        state[h] = low + [move(f"C{h}{i}", core, piece) for i, piece in enumerate(low)]

    def step_low(h):
        (low,) = mark(join(*state[h], after()))
        low = [low, move(f"Y{h}", axes(h)[0], low)]
        state[h] = low + [move(f"C{h}{i}", core, piece) for i, piece in enumerate(low)]

    def step_pair(g):
        update[g] = mark(join(update[g], spread[g], after()))[0]
        spread[g] = move(f"un{g}", z_near, update[g])

    def step_join(g):
        (both,) = mark(join(update[g], spread[g], after()))
        if U_FAR[g]:
            spread[g] = both, move(f"um{g}", z_far, both)
            return
        middle = move(f"um{g}", z_middle, both)
        spread[g] = both, middle, move(f"uo{g}", z_outer, middle)

    def step_collect(g):
        gather = join if U_FAR[g] else collect
        (mine,) = mark(gather(*spread[g], after()))
        spread[g] = mine, move(f"ux{g}", along_x, mine)

    def step_weight(mat):
        nonlocal new_weight
        g = [mat in group for group in groups].index(True)
        place = groups[g].index(mat)
        *new_weight, token = weight_step(
            weights, across, spread[g], (X_FIRST[g], U_FAR[g]), place, mat, new_weight, after()
        )
        mark([token])

    def step_basis(_):
        nonlocal bases
        *bases, token = basis(
            [piece for h in sorted(state) for piece in state[h]],
            [(X_HIGH[h], len(state[h])) for h in sorted(state)],
            across.shape[2],
            factor,
            after(),
        )
        mark([token])

    steps = {
        "cut": step_cut,
        "match": step_match,
        "project": step_project,
        "core": step_core,
        "y": step_y,
        "x": step_x,
        "far": step_far,
        "near": step_near,
        "low": step_low,
        "un": step_un,
        "pair": step_pair,
        "join": step_join,
        "collect": step_collect,
        "weight": step_weight,
        "basis": step_basis,
    }
    for entry in PLAN:
        name, which = entry.split(":")
        if name == "wait":
            pending.append(moved[which])
        else:
            steps[name](int(which))
    back = lambda x: jnp.swapaxes(x, 1, 2)[:, :, None, :]
    return (new_weight[0], back(moments[0]), back(moments[1]), jnp.swapaxes(bases[0], 0, 1))


def newton_steps(iterate, inner):
    return 1.5 * iterate - 0.5 * jnp.einsum(
        "dmr,mrs->dms", iterate, inner, precision=HIGHEST, preferred_element_type=jnp.float32
    )


def column_inner(iterate):
    return jnp.einsum(
        "dmr,dms->mrs", iterate, iterate, precision=HIGHEST, preferred_element_type=jnp.float32
    )


def per_device_any(gradients, weights, projectors, first_moment, second_moment):
    factor = math.sqrt(projectors.shape[0])
    regrouped = lax.all_to_all(gradients, "shard", split_axis=2, concat_axis=1, tiled=True)
    mats, width, cols = regrouped.shape
    rank = projectors.shape[2]
    projected = jnp.einsum(
        "dmr,mdc->mrc", projectors, regrouped, preferred_element_type=jnp.float32
    )
    first_new = 0.9 * first_moment.reshape(mats, rank, cols) + 0.1 * projected
    second_new = 0.999 * second_moment.reshape(mats, rank, cols) + 0.001 * projected * projected
    update = (first_new / CORR_FIRST / (jnp.sqrt(second_new / CORR_SECOND) + 1e-08)).astype(
        jnp.bfloat16
    )
    delta = jnp.einsum("dmr,mrc->mdc", projectors, update, preferred_element_type=jnp.float32)
    returned = lax.all_to_all(delta, "shard", split_axis=1, concat_axis=2, tiled=True)
    new_weight = weights - 0.2 * returned
    back = jnp.einsum(
        "mdc,dmr->mcr", regrouped, projectors, preferred_element_type=jnp.float32
    ).astype(jnp.bfloat16)
    partial_sum = jnp.einsum("mdc,mcr->dmr", regrouped, back, preferred_element_type=jnp.float32)
    refresh = lax.psum(partial_sum, ("shard", "tensor"))
    norms = jnp.sqrt(jnp.sum(refresh * refresh, axis=(0, 2)) + 1e-06)
    iterate = refresh / norms[None, :, None]
    for sweep in range(NS_STEPS):
        iterate = newton_steps(iterate, column_inner(iterate))
    new_basis = (iterate * factor).astype(jnp.bfloat16)
    shape_four = first_moment.shape
    return (new_weight, first_new.reshape(shape_four), second_new.reshape(shape_four), new_basis)


def solution(mesh):
    in_specs = (
        P(None, "shard", "tensor"),
        P(None, "shard", "tensor"),
        P(),
        P(None, None, "tensor", "shard"),
        P(None, None, "tensor", "shard"),
    )
    out_specs = (
        P(None, "shard", "tensor"),
        P(None, None, "tensor", "shard"),
        P(None, None, "tensor", "shard"),
        P(),
    )
    own = (mesh.shape["shard"], mesh.shape["tensor"]) == (8, 4)
    body = per_device if own else per_device_any
    return jax.shard_map(body, mesh=mesh, in_specs=in_specs, out_specs=out_specs, check_vma=False)
```

```python
import functools
import math

import jax
import jax.numpy as jnp
from jax import lax
from jax.experimental import pallas as pl
from jax.experimental.pallas import tpu as pltpu
from jax.sharding import PartitionSpec as P

NS_STEPS = 5
CORR_FIRST = 1.0
CORR_SECOND = 0.6323045752
HIGHEST = lax.Precision.HIGHEST
LANES = 128
TOKEN = jax.ShapeDtypeStruct((8, 128), jnp.float32)
GROUPS = ((0, 1), (2,))
G_X = (False, False)
X_FIRST = (False, True)
X_HIGH = (False, True)
Z_NEAR = (False, False)
U_FAR = (False, False)
JOIN_BACK = (False, False)
CUT_LIMIT = 32
COST = {"newton_schulz": 10}
PLAN = (
    "cut:0",
    "cut:1",
    "project:0",
    "project:1",
    "core:0",
    "core:1",
    "pair:1",
    "join:0",
    "y:0",
    "y:1",
    "x:0",
    "x:1",
    "collect:0",
    "far:0",
    "join:1",
    "far:1",
    "near:0",
    "near:1",
    "weight:0",
    "weight:1",
    "weight:2",
    "wait:g06",
    "basis:9",
)
def dot(a, b, dims, **kw):
    return lax.dot_general(a, b, (dims, ((), ())), preferred_element_type=jnp.float32, **kw)


def nn(a, b, **kw):
    return dot(a, b, ((1,), (0,)), **kw)


def tn(a, b, **kw):
    return dot(a, b, ((0,), (0,)), **kw)


def nt(a, b, **kw):
    return dot(a, b, ((1,), (1,)), **kw)


def block(shape, at=0):
    return pl.BlockSpec(shape, lambda i: (at,) + (0,) * (len(shape) - 1))


def call(
    kernel,
    inputs,
    in_specs,
    outs,
    out_specs=None,
    earlier=(),
    first_out=0,
    grid=1,
    after=(),
    scratch=(),
    name=None,
    us=0.5,
    limit=32,
):
    in_specs = in_specs or [block(x.shape) for x in inputs]
    out_specs = out_specs or [block(x.shape) for x in outs]
    count, unused = len(inputs), len(earlier) + len(after)

    def body(*refs):
        kernel(*refs[:count], *refs[count + unused :])

    return pl.pallas_call(
        body,
        grid=(grid,),
        in_specs=in_specs + [pl.BlockSpec(memory_space=pl.ANY)] * unused,
        out_specs=out_specs,
        out_shape=outs,
        scratch_shapes=list(scratch),
        input_output_aliases={count + i: first_out + i for i in range(len(earlier))},
        compiler_params=pltpu.CompilerParams(vmem_limit_bytes=limit * 1024 * 1024),
        cost_estimate=pl.CostEstimate(
            flops=int(us * COST.get(name, 5) * 1e9), bytes_accessed=int(us * COST.get(name, 5) * 3e6), transcendentals=0
        ),
        name=name,
    )(*inputs, *earlier, *after)


def row_owner(x_high):
    tensor = lax.axis_index("tensor")
    y, x = tensor >> 1, lax.axis_index("shard") & 1
    return (tensor & 1) * 4 + (x * 2 + y if x_high else y * 2 + x)


def fold_plan(rows, cols):
    tail = cols - LANES
    rest = 2 * tail - LANES
    stacked = -(-(rows // 2) // 16) * 8
    return tail, rest, stacked


def fold(block):
    rows, cols = block.shape
    tail, rest, stacked = fold_plan(rows, cols)
    half = rows // 2
    upper, lower = block[:half, LANES:], block[half:, LANES:]
    middle = jnp.concatenate([upper, lower[:, : tail - rest]], axis=1)
    left = lower[:, tail - rest :]
    below = jnp.concatenate(
        [left[stacked:], jnp.zeros((2 * stacked - half, rest), block.dtype)], axis=0
    )
    last = jnp.concatenate(
        [left[:stacked], below, jnp.zeros((stacked, LANES - 2 * rest), block.dtype)], axis=1
    )
    return jnp.concatenate([block[:, :LANES], middle, last], axis=0)


def unfold(folded, rows, cols):
    tail, rest, stacked = fold_plan(rows, cols)
    half = rows // 2
    middle, last = folded[rows : rows + half], folded[rows + half :]
    left = jnp.concatenate([last[:, :rest], last[: half - stacked, rest : 2 * rest]], axis=0)
    lower = jnp.concatenate([middle[:, tail:], left], axis=1)
    second = jnp.concatenate([middle[:, :tail], lower], axis=0)
    second = jnp.concatenate([second, jnp.zeros((rows, LANES - tail), folded.dtype)], axis=1)
    return jnp.concatenate([folded[:rows], second], axis=1)


def cut_kernel(cols, offsets, g_ref, *refs):
    outs, held = refs[:-1], refs[-1]
    parts, size, _ = held.shape
    for part in range(parts):
        columns = g_ref[0, :, part * cols : (part + 1) * cols].astype(jnp.float32)
        held[part] = fold(columns).astype(held.dtype)
    me = lax.axis_index("shard")
    for out, ks in zip(outs, offsets):
        for i, k in enumerate(ks):
            out[0, i * size : (i + 1) * size, :] = held[me ^ k]


def cut(gradients, group, parts, cols, offsets, after=()):
    _, rows, whole = gradients.shape
    size = folded_rows(rows, cols)
    return call(
        functools.partial(cut_kernel, cols, offsets),
        [gradients],
        [pl.BlockSpec((1, rows, whole), lambda i: (group[0] + i, 0, 0))],
        [
            jax.ShapeDtypeStruct((len(group), len(ks) * size, LANES), gradients.dtype)
            for ks in offsets
        ],
        out_specs=[
            pl.BlockSpec((1, len(ks) * size, LANES), lambda i: (i, 0, 0)) for ks in offsets
        ],
        grid=len(group),
        after=after,
        scratch=[pltpu.VMEM((parts, size, LANES), gradients.dtype)],
        name="cut_columns",
        us=len(group),
        limit=CUT_LIMIT,
    )


def match_kernel(own_ref, got_ref, *outs):
    size = outs[0].shape[1] // 2
    for k, out in enumerate(outs):
        out[:, :size, :] = own_ref[:, k * size : (k + 1) * size, :]
        out[:, size:, :] = got_ref[:, k * size : (k + 1) * size, :]


def match(own, got, count, after=()):
    shape = jax.ShapeDtypeStruct((own.shape[0], own.shape[1] // count * 2, LANES), own.dtype)
    return call(match_kernel, [own, got], None, [shape] * count, after=after, name="match", us=0.7)


def folded_rows(rows, cols):
    return rows + rows // 2 + fold_plan(rows, cols)[2]


def project_kernel(offsets, highs, rows, cols, *refs):
    count = len(offsets)
    parts = sum(len(ks) for ks in offsets)
    blocks, (p_ref, first_ref, second_ref), refs = refs[:count], refs[count : count + 3], refs[count + 3 :]
    update_ref, first_out, second_out, *terms, grad = refs
    me = lax.axis_index("shard")
    size = folded_rows(rows, cols)
    for ref, ks in zip(blocks, offsets):
        for i, k in enumerate(ks):
            part = unfold(ref[0, i * size : (i + 1) * size, :].astype(jnp.float32), rows, cols)
            grad[pl.ds(pl.multiple_of((me ^ k) * rows, rows), rows), :] = part.astype(grad.dtype)
    projected = tn(grad[...], p_ref[0])
    back = projected.astype(jnp.bfloat16)
    half = parts // 2
    for h, x_high in enumerate(highs):
        own = row_owner(x_high)
        columns = back[:, h * LANES : (h + 1) * LANES]
        for j in range(parts):
            at = pl.multiple_of((own ^ j) * rows, rows)
            terms[2 * h + j // half][j % half, 0] = nn(grad[pl.ds(at, rows), :], columns)
    projected = projected[:cols]
    first_new = 0.9 * first_ref[0] + 0.1 * projected
    second_new = 0.999 * second_ref[0] + 0.001 * projected * projected
    first_out[0] = first_new
    second_out[0] = second_new
    update_ref[0] = (
        first_new / CORR_FIRST / (jnp.sqrt(second_new / CORR_SECOND) + 1e-08)
    ).astype(jnp.bfloat16)


def project(blocks, offsets, highs, group, rows, projectors, first, second, earlier, after=()):
    mats, width, rank = projectors.shape
    cols = first.shape[1]
    parts = sum(len(ks) for ks in offsets)
    count = len(group)
    wide = -(-cols // LANES) * LANES
    of_group = lambda *shape: pl.BlockSpec((1, *shape), lambda i: (group[0] + i, 0, 0))
    own = lambda *shape: pl.BlockSpec((1, *shape), lambda i: (i, 0, 0))
    half = pl.BlockSpec((parts // 2, 1, rows, LANES), lambda i: (0, i, 0, 0))
    term = jax.ShapeDtypeStruct((parts // 2, count, rows, LANES), jnp.float32)
    number = 2 * len(highs)
    moment = of_group(cols, rank)
    return call(
        functools.partial(project_kernel, offsets, highs, rows, cols),
        [*blocks, projectors, first, second],
        [own(*b.shape[1:]) for b in blocks] + [of_group(width, rank), moment, moment],
        [
            jax.ShapeDtypeStruct((count, cols, rank), jnp.bfloat16),
            jax.ShapeDtypeStruct(first.shape, first.dtype),
            jax.ShapeDtypeStruct(second.shape, second.dtype),
        ]
        + [term] * number,
        out_specs=[own(cols, rank), moment, moment] + [half] * number,
        grid=count,
        earlier=earlier,
        first_out=1,
        after=after,
        scratch=[pltpu.VMEM((width, wide), jnp.bfloat16)],
        name="project",
        us=2 * count,
    )


def sum_kernel(terms, inputs, *refs):
    ins, outs = refs[:inputs], refs[inputs:]
    for out, parts in zip(outs, terms):
        total = None
        for which, start in parts:
            value = ins[which][start : start + out.shape[0]]
            total = value if total is None else total + value
        out[...] = total


def sums(inputs, terms, after=()):
    shapes = [(count, *inputs[0].shape[1:]) for _, count in terms]
    return call(
        functools.partial(sum_kernel, [parts for parts, _ in terms], len(inputs)),
        inputs,
        None,
        [jax.ShapeDtypeStruct(shape, jnp.float32) for shape in shapes],
        after=after,
        name="sums",
        us=0.6,
    )


def merge_kernel(count, *refs):
    ins, (sent_ref, low_ref) = refs[: 2 * count], refs[2 * count :]
    half = sent_ref.shape[0]
    at = 0
    for keep, got in zip(ins[:count], ins[count:]):
        span = slice(at, at + keep.shape[1])
        low_ref[:, span] = keep[:half] + got[:half]
        sent_ref[:, span] = keep[half:] + got[half:]
        at += keep.shape[1]


def merge(keeps, gots, after=()):
    blocks, _, rows, lanes = keeps[0].shape
    mats = sum(keep.shape[1] for keep in keeps)
    shape = jax.ShapeDtypeStruct((blocks // 2, mats, rows, lanes), jnp.float32)
    return call(
        functools.partial(merge_kernel, len(keeps)),
        [*keeps, *gots],
        None,
        [shape] * 2,
        after=after,
        name="sums",
        us=0.6,
    )


def hold_kernel(in_ref, out_ref):
    out_ref[...] = in_ref[...]


def hold(x, after=()):
    shape = jax.ShapeDtypeStruct(x.shape, x.dtype)
    return call(hold_kernel, [x], None, [shape], after=after, name="join", us=0.3)


def join_kernel(a_ref, b_ref, out_ref):
    count = a_ref.shape[0]
    out_ref[:count], out_ref[count:] = a_ref[...], b_ref[...]


def join(a, b, after=()):
    shape = jax.ShapeDtypeStruct((a.shape[0] + b.shape[0], *a.shape[1:]), a.dtype)
    return call(join_kernel, [a, b], None, [shape], after=after, name="join", us=0.4)


def collect_kernel(both_ref, middle_ref, outer_ref, out_ref):
    z = lax.axis_index("shard") >> 1
    inner = (z == 1) | (z == 2)
    out_ref[:2] = both_ref[...]

    @pl.when(inner)
    def _():
        out_ref[2:] = middle_ref[...]

    @pl.when(jnp.logical_not(inner))
    def _():
        out_ref[2:] = outer_ref[...]


def collect(both, middle, outer, after=()):
    shape = jax.ShapeDtypeStruct((4, *both.shape[1:]), both.dtype)
    return call(
        collect_kernel, [both, middle, outer], None, [shape], after=after, name="collect", us=0.6
    )


def split(a):
    high = a.astype(jnp.bfloat16)
    return high, (a - high.astype(jnp.float32)).astype(jnp.bfloat16)


def thrice(a, b):
    return nn(jnp.concatenate([a[0], a[0], a[1]], axis=1), jnp.concatenate([b[0], b[1], b[0]], axis=0))


def basis_kernel(factor, highs, *refs):
    refs, (out_ref, token_ref, held_high, held_low) = refs[:-4], refs[-4:]
    token_ref[...] = jnp.zeros_like(token_ref)
    count, width, rank = held_high.shape
    rows = width // 8
    mats = range(count)
    square, grams = [0.0] * count, []
    first = 0
    for h, (x_high, number) in enumerate(highs):
        half = refs[first : first + number]
        first += number
        own = row_owner(x_high)
        lanes = slice(h * LANES, (h + 1) * LANES)
        for j, (ref, i) in enumerate([(ref, i) for ref in half for i in range(ref.shape[0])]):
            at = pl.multiple_of((own ^ j) * rows, rows)
            for m in mats:
                value = ref[i, m]
                square[m] = square[m] + jnp.sum(value * value)
                high, low = split(value)
                held_high[m, pl.ds(at, rows), lanes] = high
                held_low[m, pl.ds(at, rows), lanes] = low
    square = [total + 1e-06 for total in square]
    eye = (
        lax.broadcasted_iota(jnp.int32, (rank, rank), 0)
        == lax.broadcasted_iota(jnp.int32, (rank, rank), 1)
    ).astype(jnp.float32)
    for m in mats:
        high, low = held_high[m], held_low[m]
        both = tn(high, jnp.concatenate([high, low], axis=1))
        cross = both[:, rank:]
        grams.append((both[:, :rank] + (cross + cross.T)) * (1.0 / square[m]))
    totals = [None] * count
    for sweep in range(NS_STEPS):
        parts = [split(gram) for gram in grams]
        if sweep < NS_STEPS - 1:
            squares = [thrice(parts[m], parts[m]) for m in mats]
        if sweep == 0:
            totals = [1.5 * eye - 0.5 * gram for gram in grams]
        else:
            totals = [1.5 * totals[m] - 0.5 * thrice(split(totals[m]), parts[m]) for m in mats]
        if sweep < NS_STEPS - 1:
            cubes = [thrice(split(squares[m]), parts[m]) for m in mats]
            grams = [2.25 * grams[m] - 1.5 * squares[m] + 0.25 * cubes[m] for m in mats]
    for m in mats:
        total = split(totals[m] * (factor / jnp.sqrt(square[m])))
        for j in range(8):
            span = slice(j * rows, (j + 1) * rows)
            value = thrice((held_high[m, span, :], held_low[m, span, :]), total)
            out_ref[m, span, :] = value.astype(jnp.bfloat16)


def basis(pieces, highs, rank, factor, after=()):
    _, count, rows, _ = pieces[0].shape
    width = 8 * rows
    return call(
        functools.partial(basis_kernel, factor, highs),
        pieces,
        None,
        [jax.ShapeDtypeStruct((count, width, rank), jnp.bfloat16), TOKEN],
        after=after,
        scratch=[pltpu.VMEM((count, width, rank), jnp.bfloat16)] * 2,
        name="newton_schulz",
        us=8,
    )


def weight_kernel(cols, x_first, far, w_ref, p_ref, *refs):
    pieces, (out_ref, token_ref, held) = refs[:-3], refs[-3:]
    token_ref[...] = jnp.zeros_like(token_ref)
    rows = w_ref.shape[1]
    me = lax.axis_index("shard")
    z, x = me >> 1, me & 1
    early = z < 2
    order = [z, z ^ 1, jnp.where(early, 2, 1), jnp.where(early, 3, 0)]
    if far:
        order = [z, z ^ 1, z ^ 2, z ^ 3]
    if x_first:
        for i in range(4):
            place = x ^ (i % 2)
            held[order[i // 2] * 2 + place] = pieces[0][i, 0]
            if far:
                held[order[2 + i // 2] * 2 + place] = pieces[1][i, 0]
                continue
            inner = (z == 1) | (z == 2)

            @pl.when(inner)
            def _(i=i, place=place):
                held[order[2 + i // 2] * 2 + place] = pieces[1][i, 0]

            @pl.when(jnp.logical_not(inner))
            def _(i=i, place=place):
                held[order[2 + i // 2] * 2 + place] = pieces[2][i, 0]

    else:
        mine_ref, other_ref = pieces
        for i in range(4):
            held[order[i] * 2 + x] = mine_ref[i, 0]
            held[order[i] * 2 + (x ^ 1)] = other_ref[i, 0]
    own = p_ref[0, pl.ds(pl.multiple_of(me * rows, rows), rows), :]
    for part in range(held.shape[0]):
        span = slice(part * cols, (part + 1) * cols)
        out_ref[0, :, span] = w_ref[0, :, span] - 0.2 * nt(own, held[part])


def weight_step(weights, projectors, pieces, modes, place, mat, earlier, after=()):
    mats, rows, whole = weights.shape
    _, width, rank = projectors.shape
    cols = pieces[0].shape[2]
    part = pl.BlockSpec((4, 1, cols, rank), lambda i: (0, place, 0, 0))
    big = block((1, rows, whole), mat)
    return call(
        functools.partial(weight_kernel, cols, *modes),
        [weights, projectors, *pieces],
        [big, block((1, width, rank), mat)] + [part] * len(pieces),
        [jax.ShapeDtypeStruct(weights.shape, weights.dtype), TOKEN],
        out_specs=[big, block(TOKEN.shape)],
        earlier=earlier,
        after=after,
        scratch=[pltpu.VMEM((8, cols, rank), jnp.bfloat16)],
        name="weight_step",
        us=1.6,
    )


def swap(x, axis, size, bit):
    return lax.ppermute(x, axis, [(i, i ^ bit) for i in range(size)])


def core(x):
    return swap(x, "tensor", 4, 1)


def along_y(x):
    return swap(x, "tensor", 4, 2)


def along_x(x):
    return swap(x, "shard", 8, 1)


def z_near(x):
    return swap(x, "shard", 8, 2)


def z_far(x):
    return swap(x, "shard", 8, 4)


def z_middle(x):
    return lax.ppermute(x, "shard", [(2, 4), (3, 5), (4, 2), (5, 3)])


def z_outer(x):
    return lax.ppermute(x, "shard", [(2, 0), (3, 1), (4, 6), (5, 7)])


def per_device(gradients, weights, projectors, first_moment, second_moment):
    factor = math.sqrt(projectors.shape[0])
    mats, rows, across_tensor = gradients.shape
    cols = across_tensor // 8
    across = jnp.swapaxes(projectors, 0, 1)
    first = jnp.swapaxes(first_moment[:, :, 0, :], 1, 2)
    second = jnp.swapaxes(second_moment[:, :, 0, :], 1, 2)
    last, pending = [], []

    def after():
        found = (*last, *pending)
        pending.clear()
        return found

    def mark(outs):
        last[:] = [outs[0]]
        return outs

    moved = {}

    def move(name, way, x):
        moved[name] = way(x)
        return moved[name]

    def axes(g):
        return (along_x, along_y) if X_HIGH[g] else (along_y, along_x)

    groups, count = GROUPS, len(GROUPS)
    moments, bases, new_weight = (), (), ()
    update, state, send, spread, kept, sent = {}, {}, {}, {}, {}, {}
    blocks, offsets = {}, {}

    def by_offset(k):
        return lambda x: swap(x, "shard", 8, k)

    def step_cut(g):
        if G_X[g]:
            own, sent = mark(cut(gradients, groups[g], 8, cols, [(0, 2, 4, 6), (1, 3, 5, 7)], after()))
            blocks[g] = own, move(f"gx{g}", along_x, sent)
            return
        offsets[g] = [(k,) for k in range(8)]
        pieces = mark(cut(gradients, groups[g], 8, cols, offsets[g], after()))
        blocks[g] = [pieces[0]] + [move(f"g{g}{k}", by_offset(k), pieces[k]) for k in range(1, 8)]

    def step_match(g):
        offsets[g] = [(k, k + 1) for k in (0, 2, 4, 6)]
        pieces = mark(match(*blocks[g], 4, after()))
        blocks[g] = [pieces[0]] + [
            move(f"g{g}{k}", by_offset(2 * k), pieces[k]) for k in range(1, 4)
        ]

    def step_project(g):
        nonlocal moments
        update[g], first_new, second_new, *terms = mark(
            project(
                blocks[g], offsets[g], X_HIGH, groups[g], rows, across, first, second, moments, after()
            )
        )
        moments = first_new, second_new
        kept[g] = terms[0::2]
        sent[g] = [move(f"c{g}{h}", core, term) for h, term in enumerate(terms[1::2])]
        update[g] = update[g][None]
        if X_FIRST[g]:
            spread[g] = move(f"ux{g}", along_x, update[g])
        elif f"un:{g}" not in PLAN:
            spread[g] = move(f"un{g}", z_near, update[g])

    def step_un(g):
        (update[g],) = mark(hold(update[g], after()))
        spread[g] = move(f"un{g}", z_near, update[g])


    def step_core(h):
        upper, state[h] = mark(
            merge([kept[g][h] for g in range(count)], [sent[g][h] for g in range(count)], after())
        )
        send[h] = move(f"y{h}", axes(h)[0], upper)

    def step_y(h):
        one, state[h] = mark(
            sums([state[h], send[h]], [([(0, 1), (1, 1)], 1), ([(0, 0), (1, 0)], 1)], after())
        )
        send[h] = move(f"x{h}", axes(h)[1], one)

    def step_x(h):
        (state[h],) = mark(sums([state[h], send[h]], [([(0, 0), (1, 0)], 1)], after()))
        send[h] = move(f"f{h}", z_near if Z_NEAR[h] else z_far, state[h])

    def step_far(h):
        (state[h],) = mark(sums([state[h], send[h]], [([(0, 0), (1, 0)], 1)], after()))
        send[h] = move(f"n{h}", z_far if Z_NEAR[h] else z_near, state[h])

    def step_near(h):
        (a,) = mark(sums([state[h], send[h]], [([(0, 0), (1, 0)], 1)], after()))
        first_way, second_way = axes(h)
        b = move(f"X{h}", second_way, a)
        if JOIN_BACK[h]:
            state[h] = a, b
            return
        low = [a, b, move(f"Y{h}", first_way, a), move(f"W{h}", first_way, b)]
        state[h] = low + [move(f"C{h}{i}", core, piece) for i, piece in enumerate(low)]

    def step_low(h):
        (low,) = mark(join(*state[h], after()))
        low = [low, move(f"Y{h}", axes(h)[0], low)]
        state[h] = low + [move(f"C{h}{i}", core, piece) for i, piece in enumerate(low)]

    def step_pair(g):
        update[g] = mark(join(update[g], spread[g], after()))[0]
        spread[g] = move(f"un{g}", z_near, update[g])

    def step_join(g):
        (both,) = mark(join(update[g], spread[g], after()))
        if U_FAR[g]:
            spread[g] = both, move(f"um{g}", z_far, both)
            return
        middle = move(f"um{g}", z_middle, both)
        spread[g] = both, middle, move(f"uo{g}", z_outer, middle)

    def step_collect(g):
        gather = join if U_FAR[g] else collect
        (mine,) = mark(gather(*spread[g], after()))
        spread[g] = mine, move(f"ux{g}", along_x, mine)

    def step_weight(mat):
        nonlocal new_weight
        g = [mat in group for group in groups].index(True)
        place = groups[g].index(mat)
        *new_weight, token = weight_step(
            weights, across, spread[g], (X_FIRST[g], U_FAR[g]), place, mat, new_weight, after()
        )
        mark([token])

    def step_basis(_):
        nonlocal bases
        *bases, token = basis(
            [piece for h in sorted(state) for piece in state[h]],
            [(X_HIGH[h], len(state[h])) for h in sorted(state)],
            across.shape[2],
            factor,
            after(),
        )
        mark([token])

    steps = {
        "cut": step_cut,
        "match": step_match,
        "project": step_project,
        "core": step_core,
        "y": step_y,
        "x": step_x,
        "far": step_far,
        "near": step_near,
        "low": step_low,
        "un": step_un,
        "pair": step_pair,
        "join": step_join,
        "collect": step_collect,
        "weight": step_weight,
        "basis": step_basis,
    }
    for entry in PLAN:
        name, which = entry.split(":")
        if name == "wait":
            pending.append(moved[which])
        else:
            steps[name](int(which))
    back = lambda x: jnp.swapaxes(x, 1, 2)[:, :, None, :]
    return (new_weight[0], back(moments[0]), back(moments[1]), jnp.swapaxes(bases[0], 0, 1))


def newton_steps(iterate, inner):
    return 1.5 * iterate - 0.5 * jnp.einsum(
        "dmr,mrs->dms", iterate, inner, precision=HIGHEST, preferred_element_type=jnp.float32
    )


def column_inner(iterate):
    return jnp.einsum(
        "dmr,dms->mrs", iterate, iterate, precision=HIGHEST, preferred_element_type=jnp.float32
    )


def per_device_any(gradients, weights, projectors, first_moment, second_moment):
    factor = math.sqrt(projectors.shape[0])
    regrouped = lax.all_to_all(gradients, "shard", split_axis=2, concat_axis=1, tiled=True)
    mats, width, cols = regrouped.shape
    rank = projectors.shape[2]
    projected = jnp.einsum(
        "dmr,mdc->mrc", projectors, regrouped, preferred_element_type=jnp.float32
    )
    first_new = 0.9 * first_moment.reshape(mats, rank, cols) + 0.1 * projected
    second_new = 0.999 * second_moment.reshape(mats, rank, cols) + 0.001 * projected * projected
    update = (first_new / CORR_FIRST / (jnp.sqrt(second_new / CORR_SECOND) + 1e-08)).astype(
        jnp.bfloat16
    )
    delta = jnp.einsum("dmr,mrc->mdc", projectors, update, preferred_element_type=jnp.float32)
    returned = lax.all_to_all(delta, "shard", split_axis=1, concat_axis=2, tiled=True)
    new_weight = weights - 0.2 * returned
    back = jnp.einsum(
        "mdc,dmr->mcr", regrouped, projectors, preferred_element_type=jnp.float32
    ).astype(jnp.bfloat16)
    partial_sum = jnp.einsum("mdc,mcr->dmr", regrouped, back, preferred_element_type=jnp.float32)
    refresh = lax.psum(partial_sum, ("shard", "tensor"))
    norms = jnp.sqrt(jnp.sum(refresh * refresh, axis=(0, 2)) + 1e-06)
    iterate = refresh / norms[None, :, None]
    for sweep in range(NS_STEPS):
        iterate = newton_steps(iterate, column_inner(iterate))
    new_basis = (iterate * factor).astype(jnp.bfloat16)
    shape_four = first_moment.shape
    return (new_weight, first_new.reshape(shape_four), second_new.reshape(shape_four), new_basis)


def solution(mesh):
    in_specs = (
        P(None, "shard", "tensor"),
        P(None, "shard", "tensor"),
        P(),
        P(None, None, "tensor", "shard"),
        P(None, None, "tensor", "shard"),
    )
    out_specs = (
        P(None, "shard", "tensor"),
        P(None, None, "tensor", "shard"),
        P(None, None, "tensor", "shard"),
        P(),
    )
    own = (mesh.shape["shard"], mesh.shape["tensor"]) == (8, 4)
    body = per_device if own else per_device_any
    return jax.shard_map(body, mesh=mesh, in_specs=in_specs, out_specs=out_specs, check_vma=False)
```

```python
import functools
import math

import jax
import jax.numpy as jnp
from jax import lax
from jax.experimental import pallas as pl
from jax.experimental.pallas import tpu as pltpu
from jax.sharding import PartitionSpec as P

NS_STEPS = 5
CORR_FIRST = 1.0
CORR_SECOND = 0.6323045752
HIGHEST = lax.Precision.HIGHEST
LANES = 128
TOKEN = jax.ShapeDtypeStruct((8, 128), jnp.float32)
GROUPS = ((0, 1), (2,))
G_X = (False, False)
X_FIRST = (False, True)
X_HIGH = (False, True)
Z_NEAR = (False, False)
U_FAR = (False, False)
JOIN_BACK = (True, True)
CUT_LIMIT = 32
COST = {"newton_schulz": 10}
PLAN = (
    "cut:0",
    "cut:1",
    "project:0",
    "project:1",
    "core:0",
    "core:1",
    "pair:1",
    "join:0",
    "y:0",
    "y:1",
    "x:0",
    "x:1",
    "collect:0",
    "far:0",
    "join:1",
    "far:1",
    "near:0",
    "near:1",
    "weight:0",
    "low:0",
    "low:1",
    "weight:1",
    "weight:2",
    "wait:g06",
    "basis:9",
)
def dot(a, b, dims, **kw):
    return lax.dot_general(a, b, (dims, ((), ())), preferred_element_type=jnp.float32, **kw)


def nn(a, b, **kw):
    return dot(a, b, ((1,), (0,)), **kw)


def tn(a, b, **kw):
    return dot(a, b, ((0,), (0,)), **kw)


def nt(a, b, **kw):
    return dot(a, b, ((1,), (1,)), **kw)


def block(shape, at=0):
    return pl.BlockSpec(shape, lambda i: (at,) + (0,) * (len(shape) - 1))


def call(
    kernel,
    inputs,
    in_specs,
    outs,
    out_specs=None,
    earlier=(),
    first_out=0,
    grid=1,
    after=(),
    scratch=(),
    name=None,
    us=0.5,
    limit=32,
):
    in_specs = in_specs or [block(x.shape) for x in inputs]
    out_specs = out_specs or [block(x.shape) for x in outs]
    count, unused = len(inputs), len(earlier) + len(after)

    def body(*refs):
        kernel(*refs[:count], *refs[count + unused :])

    return pl.pallas_call(
        body,
        grid=(grid,),
        in_specs=in_specs + [pl.BlockSpec(memory_space=pl.ANY)] * unused,
        out_specs=out_specs,
        out_shape=outs,
        scratch_shapes=list(scratch),
        input_output_aliases={count + i: first_out + i for i in range(len(earlier))},
        compiler_params=pltpu.CompilerParams(vmem_limit_bytes=limit * 1024 * 1024),
        cost_estimate=pl.CostEstimate(
            flops=int(us * COST.get(name, 5) * 1e9), bytes_accessed=int(us * COST.get(name, 5) * 3e6), transcendentals=0
        ),
        name=name,
    )(*inputs, *earlier, *after)


def row_owner(x_high):
    tensor = lax.axis_index("tensor")
    y, x = tensor >> 1, lax.axis_index("shard") & 1
    return (tensor & 1) * 4 + (x * 2 + y if x_high else y * 2 + x)


def fold_plan(rows, cols):
    tail = cols - LANES
    rest = 2 * tail - LANES
    stacked = -(-(rows // 2) // 16) * 8
    return tail, rest, stacked


def fold(block):
    rows, cols = block.shape
    tail, rest, stacked = fold_plan(rows, cols)
    half = rows // 2
    upper, lower = block[:half, LANES:], block[half:, LANES:]
    middle = jnp.concatenate([upper, lower[:, : tail - rest]], axis=1)
    left = lower[:, tail - rest :]
    below = jnp.concatenate(
        [left[stacked:], jnp.zeros((2 * stacked - half, rest), block.dtype)], axis=0
    )
    last = jnp.concatenate(
        [left[:stacked], below, jnp.zeros((stacked, LANES - 2 * rest), block.dtype)], axis=1
    )
    return jnp.concatenate([block[:, :LANES], middle, last], axis=0)


def unfold(folded, rows, cols):
    tail, rest, stacked = fold_plan(rows, cols)
    half = rows // 2
    middle, last = folded[rows : rows + half], folded[rows + half :]
    left = jnp.concatenate([last[:, :rest], last[: half - stacked, rest : 2 * rest]], axis=0)
    lower = jnp.concatenate([middle[:, tail:], left], axis=1)
    second = jnp.concatenate([middle[:, :tail], lower], axis=0)
    second = jnp.concatenate([second, jnp.zeros((rows, LANES - tail), folded.dtype)], axis=1)
    return jnp.concatenate([folded[:rows], second], axis=1)


def cut_kernel(cols, offsets, g_ref, *refs):
    outs, held = refs[:-1], refs[-1]
    parts, size, _ = held.shape
    for part in range(parts):
        columns = g_ref[0, :, part * cols : (part + 1) * cols].astype(jnp.float32)
        held[part] = fold(columns).astype(held.dtype)
    me = lax.axis_index("shard")
    for out, ks in zip(outs, offsets):
        for i, k in enumerate(ks):
            out[0, i * size : (i + 1) * size, :] = held[me ^ k]


def cut(gradients, group, parts, cols, offsets, after=()):
    _, rows, whole = gradients.shape
    size = folded_rows(rows, cols)
    return call(
        functools.partial(cut_kernel, cols, offsets),
        [gradients],
        [pl.BlockSpec((1, rows, whole), lambda i: (group[0] + i, 0, 0))],
        [
            jax.ShapeDtypeStruct((len(group), len(ks) * size, LANES), gradients.dtype)
            for ks in offsets
        ],
        out_specs=[
            pl.BlockSpec((1, len(ks) * size, LANES), lambda i: (i, 0, 0)) for ks in offsets
        ],
        grid=len(group),
        after=after,
        scratch=[pltpu.VMEM((parts, size, LANES), gradients.dtype)],
        name="cut_columns",
        us=len(group),
        limit=CUT_LIMIT,
    )


def match_kernel(own_ref, got_ref, *outs):
    size = outs[0].shape[1] // 2
    for k, out in enumerate(outs):
        out[:, :size, :] = own_ref[:, k * size : (k + 1) * size, :]
        out[:, size:, :] = got_ref[:, k * size : (k + 1) * size, :]


def match(own, got, count, after=()):
    shape = jax.ShapeDtypeStruct((own.shape[0], own.shape[1] // count * 2, LANES), own.dtype)
    return call(match_kernel, [own, got], None, [shape] * count, after=after, name="match", us=0.7)


def folded_rows(rows, cols):
    return rows + rows // 2 + fold_plan(rows, cols)[2]


def project_kernel(offsets, highs, rows, cols, *refs):
    count = len(offsets)
    parts = sum(len(ks) for ks in offsets)
    blocks, (p_ref, first_ref, second_ref), refs = refs[:count], refs[count : count + 3], refs[count + 3 :]
    update_ref, first_out, second_out, *terms, grad = refs
    me = lax.axis_index("shard")
    size = folded_rows(rows, cols)
    for ref, ks in zip(blocks, offsets):
        for i, k in enumerate(ks):
            part = unfold(ref[0, i * size : (i + 1) * size, :].astype(jnp.float32), rows, cols)
            grad[pl.ds(pl.multiple_of((me ^ k) * rows, rows), rows), :] = part.astype(grad.dtype)
    projected = tn(grad[...], p_ref[0])
    back = projected.astype(jnp.bfloat16)
    half = parts // 2
    for h, x_high in enumerate(highs):
        own = row_owner(x_high)
        columns = back[:, h * LANES : (h + 1) * LANES]
        for j in range(parts):
            at = pl.multiple_of((own ^ j) * rows, rows)
            terms[2 * h + j // half][j % half, 0] = nn(grad[pl.ds(at, rows), :], columns)
    projected = projected[:cols]
    first_new = 0.9 * first_ref[0] + 0.1 * projected
    second_new = 0.999 * second_ref[0] + 0.001 * projected * projected
    first_out[0] = first_new
    second_out[0] = second_new
    update_ref[0] = (
        first_new / CORR_FIRST / (jnp.sqrt(second_new / CORR_SECOND) + 1e-08)
    ).astype(jnp.bfloat16)


def project(blocks, offsets, highs, group, rows, projectors, first, second, earlier, after=()):
    mats, width, rank = projectors.shape
    cols = first.shape[1]
    parts = sum(len(ks) for ks in offsets)
    count = len(group)
    wide = -(-cols // LANES) * LANES
    of_group = lambda *shape: pl.BlockSpec((1, *shape), lambda i: (group[0] + i, 0, 0))
    own = lambda *shape: pl.BlockSpec((1, *shape), lambda i: (i, 0, 0))
    half = pl.BlockSpec((parts // 2, 1, rows, LANES), lambda i: (0, i, 0, 0))
    term = jax.ShapeDtypeStruct((parts // 2, count, rows, LANES), jnp.float32)
    number = 2 * len(highs)
    moment = of_group(cols, rank)
    return call(
        functools.partial(project_kernel, offsets, highs, rows, cols),
        [*blocks, projectors, first, second],
        [own(*b.shape[1:]) for b in blocks] + [of_group(width, rank), moment, moment],
        [
            jax.ShapeDtypeStruct((count, cols, rank), jnp.bfloat16),
            jax.ShapeDtypeStruct(first.shape, first.dtype),
            jax.ShapeDtypeStruct(second.shape, second.dtype),
        ]
        + [term] * number,
        out_specs=[own(cols, rank), moment, moment] + [half] * number,
        grid=count,
        earlier=earlier,
        first_out=1,
        after=after,
        scratch=[pltpu.VMEM((width, wide), jnp.bfloat16)],
        name="project",
        us=2 * count,
    )


def sum_kernel(terms, inputs, *refs):
    ins, outs = refs[:inputs], refs[inputs:]
    for out, parts in zip(outs, terms):
        total = None
        for which, start in parts:
            value = ins[which][start : start + out.shape[0]]
            total = value if total is None else total + value
        out[...] = total


def sums(inputs, terms, after=()):
    shapes = [(count, *inputs[0].shape[1:]) for _, count in terms]
    return call(
        functools.partial(sum_kernel, [parts for parts, _ in terms], len(inputs)),
        inputs,
        None,
        [jax.ShapeDtypeStruct(shape, jnp.float32) for shape in shapes],
        after=after,
        name="sums",
        us=0.6,
    )


def merge_kernel(count, *refs):
    ins, (sent_ref, low_ref) = refs[: 2 * count], refs[2 * count :]
    half = sent_ref.shape[0]
    at = 0
    for keep, got in zip(ins[:count], ins[count:]):
        span = slice(at, at + keep.shape[1])
        low_ref[:, span] = keep[:half] + got[:half]
        sent_ref[:, span] = keep[half:] + got[half:]
        at += keep.shape[1]


def merge(keeps, gots, after=()):
    blocks, _, rows, lanes = keeps[0].shape
    mats = sum(keep.shape[1] for keep in keeps)
    shape = jax.ShapeDtypeStruct((blocks // 2, mats, rows, lanes), jnp.float32)
    return call(
        functools.partial(merge_kernel, len(keeps)),
        [*keeps, *gots],
        None,
        [shape] * 2,
        after=after,
        name="sums",
        us=0.6,
    )


def hold_kernel(in_ref, out_ref):
    out_ref[...] = in_ref[...]


def hold(x, after=()):
    shape = jax.ShapeDtypeStruct(x.shape, x.dtype)
    return call(hold_kernel, [x], None, [shape], after=after, name="join", us=0.3)


def join_kernel(a_ref, b_ref, out_ref):
    count = a_ref.shape[0]
    out_ref[:count], out_ref[count:] = a_ref[...], b_ref[...]


def join(a, b, after=()):
    shape = jax.ShapeDtypeStruct((a.shape[0] + b.shape[0], *a.shape[1:]), a.dtype)
    return call(join_kernel, [a, b], None, [shape], after=after, name="join", us=0.4)


def collect_kernel(both_ref, middle_ref, outer_ref, out_ref):
    z = lax.axis_index("shard") >> 1
    inner = (z == 1) | (z == 2)
    out_ref[:2] = both_ref[...]

    @pl.when(inner)
    def _():
        out_ref[2:] = middle_ref[...]

    @pl.when(jnp.logical_not(inner))
    def _():
        out_ref[2:] = outer_ref[...]


def collect(both, middle, outer, after=()):
    shape = jax.ShapeDtypeStruct((4, *both.shape[1:]), both.dtype)
    return call(
        collect_kernel, [both, middle, outer], None, [shape], after=after, name="collect", us=0.6
    )


def split(a):
    high = a.astype(jnp.bfloat16)
    return high, (a - high.astype(jnp.float32)).astype(jnp.bfloat16)


def thrice(a, b):
    return nn(jnp.concatenate([a[0], a[0], a[1]], axis=1), jnp.concatenate([b[0], b[1], b[0]], axis=0))


def basis_kernel(factor, highs, *refs):
    refs, (out_ref, token_ref, held_high, held_low) = refs[:-4], refs[-4:]
    token_ref[...] = jnp.zeros_like(token_ref)
    count, width, rank = held_high.shape
    rows = width // 8
    mats = range(count)
    square, grams = [0.0] * count, []
    first = 0
    for h, (x_high, number) in enumerate(highs):
        half = refs[first : first + number]
        first += number
        own = row_owner(x_high)
        lanes = slice(h * LANES, (h + 1) * LANES)
        for j, (ref, i) in enumerate([(ref, i) for ref in half for i in range(ref.shape[0])]):
            at = pl.multiple_of((own ^ j) * rows, rows)
            for m in mats:
                value = ref[i, m]
                square[m] = square[m] + jnp.sum(value * value)
                high, low = split(value)
                held_high[m, pl.ds(at, rows), lanes] = high
                held_low[m, pl.ds(at, rows), lanes] = low
    square = [total + 1e-06 for total in square]
    eye = (
        lax.broadcasted_iota(jnp.int32, (rank, rank), 0)
        == lax.broadcasted_iota(jnp.int32, (rank, rank), 1)
    ).astype(jnp.float32)
    for m in mats:
        high, low = held_high[m], held_low[m]
        both = tn(high, jnp.concatenate([high, low], axis=1))
        cross = both[:, rank:]
        grams.append((both[:, :rank] + (cross + cross.T)) * (1.0 / square[m]))
    totals = [None] * count
    for sweep in range(NS_STEPS):
        parts = [split(gram) for gram in grams]
        if sweep < NS_STEPS - 1:
            squares = [thrice(parts[m], parts[m]) for m in mats]
        if sweep == 0:
            totals = [1.5 * eye - 0.5 * gram for gram in grams]
        else:
            totals = [1.5 * totals[m] - 0.5 * thrice(split(totals[m]), parts[m]) for m in mats]
        if sweep < NS_STEPS - 1:
            cubes = [thrice(split(squares[m]), parts[m]) for m in mats]
            grams = [2.25 * grams[m] - 1.5 * squares[m] + 0.25 * cubes[m] for m in mats]
    for m in mats:
        total = split(totals[m] * (factor / jnp.sqrt(square[m])))
        for j in range(8):
            span = slice(j * rows, (j + 1) * rows)
            value = thrice((held_high[m, span, :], held_low[m, span, :]), total)
            out_ref[m, span, :] = value.astype(jnp.bfloat16)


def basis(pieces, highs, rank, factor, after=()):
    _, count, rows, _ = pieces[0].shape
    width = 8 * rows
    return call(
        functools.partial(basis_kernel, factor, highs),
        pieces,
        None,
        [jax.ShapeDtypeStruct((count, width, rank), jnp.bfloat16), TOKEN],
        after=after,
        scratch=[pltpu.VMEM((count, width, rank), jnp.bfloat16)] * 2,
        name="newton_schulz",
        us=8,
    )


def weight_kernel(cols, x_first, far, w_ref, p_ref, *refs):
    pieces, (out_ref, token_ref, held) = refs[:-3], refs[-3:]
    token_ref[...] = jnp.zeros_like(token_ref)
    rows = w_ref.shape[1]
    me = lax.axis_index("shard")
    z, x = me >> 1, me & 1
    early = z < 2
    order = [z, z ^ 1, jnp.where(early, 2, 1), jnp.where(early, 3, 0)]
    if far:
        order = [z, z ^ 1, z ^ 2, z ^ 3]
    if x_first:
        for i in range(4):
            place = x ^ (i % 2)
            held[order[i // 2] * 2 + place] = pieces[0][i, 0]
            if far:
                held[order[2 + i // 2] * 2 + place] = pieces[1][i, 0]
                continue
            inner = (z == 1) | (z == 2)

            @pl.when(inner)
            def _(i=i, place=place):
                held[order[2 + i // 2] * 2 + place] = pieces[1][i, 0]

            @pl.when(jnp.logical_not(inner))
            def _(i=i, place=place):
                held[order[2 + i // 2] * 2 + place] = pieces[2][i, 0]

    else:
        mine_ref, other_ref = pieces
        for i in range(4):
            held[order[i] * 2 + x] = mine_ref[i, 0]
            held[order[i] * 2 + (x ^ 1)] = other_ref[i, 0]
    own = p_ref[0, pl.ds(pl.multiple_of(me * rows, rows), rows), :]
    for part in range(held.shape[0]):
        span = slice(part * cols, (part + 1) * cols)
        out_ref[0, :, span] = w_ref[0, :, span] - 0.2 * nt(own, held[part])


def weight_step(weights, projectors, pieces, modes, place, mat, earlier, after=()):
    mats, rows, whole = weights.shape
    _, width, rank = projectors.shape
    cols = pieces[0].shape[2]
    part = pl.BlockSpec((4, 1, cols, rank), lambda i: (0, place, 0, 0))
    big = block((1, rows, whole), mat)
    return call(
        functools.partial(weight_kernel, cols, *modes),
        [weights, projectors, *pieces],
        [big, block((1, width, rank), mat)] + [part] * len(pieces),
        [jax.ShapeDtypeStruct(weights.shape, weights.dtype), TOKEN],
        out_specs=[big, block(TOKEN.shape)],
        earlier=earlier,
        after=after,
        scratch=[pltpu.VMEM((8, cols, rank), jnp.bfloat16)],
        name="weight_step",
        us=1.6,
    )


def swap(x, axis, size, bit):
    return lax.ppermute(x, axis, [(i, i ^ bit) for i in range(size)])


def core(x):
    return swap(x, "tensor", 4, 1)


def along_y(x):
    return swap(x, "tensor", 4, 2)


def along_x(x):
    return swap(x, "shard", 8, 1)


def z_near(x):
    return swap(x, "shard", 8, 2)


def z_far(x):
    return swap(x, "shard", 8, 4)


def z_middle(x):
    return lax.ppermute(x, "shard", [(2, 4), (3, 5), (4, 2), (5, 3)])


def z_outer(x):
    return lax.ppermute(x, "shard", [(2, 0), (3, 1), (4, 6), (5, 7)])


def per_device(gradients, weights, projectors, first_moment, second_moment):
    factor = math.sqrt(projectors.shape[0])
    mats, rows, across_tensor = gradients.shape
    cols = across_tensor // 8
    across = jnp.swapaxes(projectors, 0, 1)
    first = jnp.swapaxes(first_moment[:, :, 0, :], 1, 2)
    second = jnp.swapaxes(second_moment[:, :, 0, :], 1, 2)
    last, pending = [], []

    def after():
        found = (*last, *pending)
        pending.clear()
        return found

    def mark(outs):
        last[:] = [outs[0]]
        return outs

    moved = {}

    def move(name, way, x):
        moved[name] = way(x)
        return moved[name]

    def axes(g):
        return (along_x, along_y) if X_HIGH[g] else (along_y, along_x)

    groups, count = GROUPS, len(GROUPS)
    moments, bases, new_weight = (), (), ()
    update, state, send, spread, kept, sent = {}, {}, {}, {}, {}, {}
    blocks, offsets = {}, {}

    def by_offset(k):
        return lambda x: swap(x, "shard", 8, k)

    def step_cut(g):
        if G_X[g]:
            own, sent = mark(cut(gradients, groups[g], 8, cols, [(0, 2, 4, 6), (1, 3, 5, 7)], after()))
            blocks[g] = own, move(f"gx{g}", along_x, sent)
            return
        offsets[g] = [(k,) for k in range(8)]
        pieces = mark(cut(gradients, groups[g], 8, cols, offsets[g], after()))
        blocks[g] = [pieces[0]] + [move(f"g{g}{k}", by_offset(k), pieces[k]) for k in range(1, 8)]

    def step_match(g):
        offsets[g] = [(k, k + 1) for k in (0, 2, 4, 6)]
        pieces = mark(match(*blocks[g], 4, after()))
        blocks[g] = [pieces[0]] + [
            move(f"g{g}{k}", by_offset(2 * k), pieces[k]) for k in range(1, 4)
        ]

    def step_project(g):
        nonlocal moments
        update[g], first_new, second_new, *terms = mark(
            project(
                blocks[g], offsets[g], X_HIGH, groups[g], rows, across, first, second, moments, after()
            )
        )
        moments = first_new, second_new
        kept[g] = terms[0::2]
        sent[g] = [move(f"c{g}{h}", core, term) for h, term in enumerate(terms[1::2])]
        update[g] = update[g][None]
        if X_FIRST[g]:
            spread[g] = move(f"ux{g}", along_x, update[g])
        elif f"un:{g}" not in PLAN:
            spread[g] = move(f"un{g}", z_near, update[g])

    def step_un(g):
        (update[g],) = mark(hold(update[g], after()))
        spread[g] = move(f"un{g}", z_near, update[g])


    def step_core(h):
        upper, state[h] = mark(
            merge([kept[g][h] for g in range(count)], [sent[g][h] for g in range(count)], after())
        )
        send[h] = move(f"y{h}", axes(h)[0], upper)

    def step_y(h):
        one, state[h] = mark(
            sums([state[h], send[h]], [([(0, 1), (1, 1)], 1), ([(0, 0), (1, 0)], 1)], after())
        )
        send[h] = move(f"x{h}", axes(h)[1], one)

    def step_x(h):
        (state[h],) = mark(sums([state[h], send[h]], [([(0, 0), (1, 0)], 1)], after()))
        send[h] = move(f"f{h}", z_near if Z_NEAR[h] else z_far, state[h])

    def step_far(h):
        (state[h],) = mark(sums([state[h], send[h]], [([(0, 0), (1, 0)], 1)], after()))
        send[h] = move(f"n{h}", z_far if Z_NEAR[h] else z_near, state[h])

    def step_near(h):
        (a,) = mark(sums([state[h], send[h]], [([(0, 0), (1, 0)], 1)], after()))
        first_way, second_way = axes(h)
        b = move(f"X{h}", second_way, a)
        if JOIN_BACK[h]:
            state[h] = a, b
            return
        low = [a, b, move(f"Y{h}", first_way, a), move(f"W{h}", first_way, b)]
        state[h] = low + [move(f"C{h}{i}", core, piece) for i, piece in enumerate(low)]

    def step_low(h):
        (low,) = mark(join(*state[h], after()))
        low = [low, move(f"Y{h}", axes(h)[0], low)]
        state[h] = low + [move(f"C{h}{i}", core, piece) for i, piece in enumerate(low)]

    def step_pair(g):
        update[g] = mark(join(update[g], spread[g], after()))[0]
        spread[g] = move(f"un{g}", z_near, update[g])

    def step_join(g):
        (both,) = mark(join(update[g], spread[g], after()))
        if U_FAR[g]:
            spread[g] = both, move(f"um{g}", z_far, both)
            return
        middle = move(f"um{g}", z_middle, both)
        spread[g] = both, middle, move(f"uo{g}", z_outer, middle)

    def step_collect(g):
        gather = join if U_FAR[g] else collect
        (mine,) = mark(gather(*spread[g], after()))
        spread[g] = mine, move(f"ux{g}", along_x, mine)

    def step_weight(mat):
        nonlocal new_weight
        g = [mat in group for group in groups].index(True)
        place = groups[g].index(mat)
        *new_weight, token = weight_step(
            weights, across, spread[g], (X_FIRST[g], U_FAR[g]), place, mat, new_weight, after()
        )
        mark([token])

    def step_basis(_):
        nonlocal bases
        *bases, token = basis(
            [piece for h in sorted(state) for piece in state[h]],
            [(X_HIGH[h], len(state[h])) for h in sorted(state)],
            across.shape[2],
            factor,
            after(),
        )
        mark([token])

    steps = {
        "cut": step_cut,
        "match": step_match,
        "project": step_project,
        "core": step_core,
        "y": step_y,
        "x": step_x,
        "far": step_far,
        "near": step_near,
        "low": step_low,
        "un": step_un,
        "pair": step_pair,
        "join": step_join,
        "collect": step_collect,
        "weight": step_weight,
        "basis": step_basis,
    }
    for entry in PLAN:
        name, which = entry.split(":")
        if name == "wait":
            pending.append(moved[which])
        else:
            steps[name](int(which))
    back = lambda x: jnp.swapaxes(x, 1, 2)[:, :, None, :]
    return (new_weight[0], back(moments[0]), back(moments[1]), jnp.swapaxes(bases[0], 0, 1))


def newton_steps(iterate, inner):
    return 1.5 * iterate - 0.5 * jnp.einsum(
        "dmr,mrs->dms", iterate, inner, precision=HIGHEST, preferred_element_type=jnp.float32
    )


def column_inner(iterate):
    return jnp.einsum(
        "dmr,dms->mrs", iterate, iterate, precision=HIGHEST, preferred_element_type=jnp.float32
    )


def per_device_any(gradients, weights, projectors, first_moment, second_moment):
    factor = math.sqrt(projectors.shape[0])
    regrouped = lax.all_to_all(gradients, "shard", split_axis=2, concat_axis=1, tiled=True)
    mats, width, cols = regrouped.shape
    rank = projectors.shape[2]
    projected = jnp.einsum(
        "dmr,mdc->mrc", projectors, regrouped, preferred_element_type=jnp.float32
    )
    first_new = 0.9 * first_moment.reshape(mats, rank, cols) + 0.1 * projected
    second_new = 0.999 * second_moment.reshape(mats, rank, cols) + 0.001 * projected * projected
    update = (first_new / CORR_FIRST / (jnp.sqrt(second_new / CORR_SECOND) + 1e-08)).astype(
        jnp.bfloat16
    )
    delta = jnp.einsum("dmr,mrc->mdc", projectors, update, preferred_element_type=jnp.float32)
    returned = lax.all_to_all(delta, "shard", split_axis=1, concat_axis=2, tiled=True)
    new_weight = weights - 0.2 * returned
    back = jnp.einsum(
        "mdc,dmr->mcr", regrouped, projectors, preferred_element_type=jnp.float32
    ).astype(jnp.bfloat16)
    partial_sum = jnp.einsum("mdc,mcr->dmr", regrouped, back, preferred_element_type=jnp.float32)
    refresh = lax.psum(partial_sum, ("shard", "tensor"))
    norms = jnp.sqrt(jnp.sum(refresh * refresh, axis=(0, 2)) + 1e-06)
    iterate = refresh / norms[None, :, None]
    for sweep in range(NS_STEPS):
        iterate = newton_steps(iterate, column_inner(iterate))
    new_basis = (iterate * factor).astype(jnp.bfloat16)
    shape_four = first_moment.shape
    return (new_weight, first_new.reshape(shape_four), second_new.reshape(shape_four), new_basis)


def solution(mesh):
    in_specs = (
        P(None, "shard", "tensor"),
        P(None, "shard", "tensor"),
        P(),
        P(None, None, "tensor", "shard"),
        P(None, None, "tensor", "shard"),
    )
    out_specs = (
        P(None, "shard", "tensor"),
        P(None, None, "tensor", "shard"),
        P(None, None, "tensor", "shard"),
        P(),
    )
    own = (mesh.shape["shard"], mesh.shape["tensor"]) == (8, 4)
    body = per_device if own else per_device_any
    return jax.shard_map(body, mesh=mesh, in_specs=in_specs, out_specs=out_specs, check_vma=False)
```
